32 devices in a mesh: field: 2 (over y), expo: 8 (over z, core), strip: 2 (over x).
Axes of the slice: x: 2, y: 2, z: 4, core: 2. Of those that a mesh axis runs over, the one named last changes fastest.
Arguments:
- science: bfloat16 [128, 64, 512], P(('field', 'expo'), 'strip'), parts along dimension 0, may hold values from -6 to 6
- inv_var: bfloat16 [128, 64, 512], P(('field', 'expo'), 'strip'), parts along dimension 0, may hold values from 0.25 to 4
- psf_rows: float32 [128, 9], P(('field', 'expo')), parts along dimension 0, may hold values from 0.2 to 1
- psf_cols: float32 [128, 9], P(('field', 'expo')), parts along dimension 0, may hold values from 0.2 to 1
- row_shift: int32 [128, 8], P(('field', 'expo')), parts along dimension 0, may hold values from 0 to 16
- col_shift: int32 [128, 8], P(('field', 'expo')), parts along dimension 0, may hold values from -16 to 16
- exposure_ok: int32 [128], P(('field', 'expo')), parts along dimension 0, may hold values 0 or 1
Outputs:
- likelihood: float32 [2, 16, 32, 512], P('strip', 'field', 'expo'), parts along dimension 1
The draws below stay inside these ranges and needn't reach their ends.
There are 2 independent parts, one for each index of `field`. The reference program is written for one: setup_inputs(seed, part) draws one part's arguments, and reference() takes and returns one part's arrays. A program takes and returns all parts, laid end to end along the dimension named above; each array names one. Nothing has to cross between parts.
Inputs may be any that keep to these rules, and one draw needn't show every extreme that they name: `row_shift`: every shift lies in 0..16, so S[e, v, r] reads map rows r to r + 16 only, never lower rows.
All inputs are finite; a program needn't handle non-finite values. No bound on the sum of `exposure_ok` on one device may be relied on, other than what follows from the above.
Results may differ from the reference program's by a relative error of at most 0.0017.
Values may be sent and summed in bfloat16 or wider, within the bound.
A program may use at most 64 MiB of HBM per device.

```python
import math
import jax
import jax.numpy as jnp
from jax import lax

COLS = 512
VELS = 8
PSF_RAD = 4
TAPS = 9
SHIFT = 16
ROWS_DEV = 32
EXPOSURES = 64
ROWS = 64
N_STRIP = 2


def place_ends(drawn, stream_key, least, top_value):
    longest = drawn.shape.index(max(drawn.shape))
    spots = []
    for shift in (0, 1):
        where = [jax.random.randint(jax.random.fold_in(stream_key, axis), (), 0, length) for axis, length in enumerate(drawn.shape)]
        where[longest] = (where[longest] + shift) % drawn.shape[longest]
        spots.append(tuple(where))
    return drawn.at[spots[0]].set(least).at[spots[1]].set(top_value)


def block_levels(own_key, extent, pieces, least, largest):
    def one(dim, shards_of):
        steps = jax.random.uniform(jax.random.fold_in(jax.random.fold_in(own_key, 6), dim), (shards_of,), jnp.float32, least / len(pieces), largest / len(pieces))
        return jnp.repeat(jnp.exp(steps), extent[dim] // shards_of).reshape((-1,) + (1,) * (len(extent) - dim - 1))

    gain = one(*pieces[0])
    for cut in pieces[1:]:
        gain = gain * one(*cut)
    return gain


def noise(stream_key, extent, spread, limit, split=(), dtype=jnp.bfloat16):
    loudness = block_levels(stream_key, extent, split, -0.22, 0.18) if split else 1.0
    array = jax.random.normal(stream_key, extent, jnp.float32) * spread * loudness
    return jnp.minimum(jnp.maximum(array, -limit), limit).astype(dtype)


def setup_inputs(seed: int = 0, part: int = 0) -> dict:
    key_list = jax.random.split(jax.random.key(seed), 8)
    own_keys = jax.random.split(jax.random.fold_in(key_list[7], part), 8)
    science = noise(own_keys[0], (EXPOSURES, ROWS, COLS), 1.0, 6.0, ((0, 8), (1, 2)))
    inv_var = jnp.clip(jnp.exp(math.log(4.0) - 2.7725887 * jax.random.uniform(own_keys[1], (EXPOSURES, ROWS, COLS), jnp.float32) ** block_levels(own_keys[1], (EXPOSURES, ROWS, COLS), ((0, 8), (1, 2)), -0.2, 0.2)), 0.25, 4.0).astype(jnp.bfloat16)
    psf_rows = jnp.clip(0.2 + 0.8 * jax.random.uniform(own_keys[2], (EXPOSURES, TAPS), jnp.float32) ** block_levels(own_keys[2], (EXPOSURES, TAPS), ((0, 8),), -0.2, 0.2), 0.2, 1.0)
    psf_cols = jnp.clip(0.2 + 0.8 * jax.random.uniform(own_keys[3], (EXPOSURES, TAPS), jnp.float32) ** block_levels(own_keys[3], (EXPOSURES, TAPS), ((0, 8),), -0.2, 0.2), 0.2, 1.0)
    row_shift = place_ends(jax.random.randint(own_keys[4], (EXPOSURES, VELS), 0, SHIFT + 1), jax.random.fold_in(own_keys[4], 1), 0, SHIFT).astype(jnp.int32)
    col_shift = place_ends(jax.random.randint(own_keys[5], (EXPOSURES, VELS), 0 - SHIFT, SHIFT + 1), jax.random.fold_in(own_keys[5], 1), 0 - SHIFT, SHIFT).astype(jnp.int32)
    exposure_ok = place_ends((jax.random.randint(own_keys[6], (EXPOSURES,), 0, 4) < 3).astype(jnp.int32), jax.random.fold_in(own_keys[6], 1), 0, 1)
    return dict(science=science, inv_var=inv_var, psf_rows=psf_rows, psf_cols=psf_cols, row_shift=row_shift, col_shift=col_shift, exposure_ok=exposure_ok)


def filter_one(picture, row_taps, col_taps, out_rows):
    columns = picture.shape[2]
    tap_count = row_taps.shape[1]
    radius = tap_count // 2
    padded = jnp.pad(picture, ((0, 0), (0, 0), (radius, radius)))
    colpass = col_taps[:, 0, None, None] * padded[:, :, 0:columns]
    for b in range(1, tap_count):
        colpass = colpass + col_taps[:, b, None, None] * padded[:, :, b:b + columns]
    result = row_taps[:, 0, None, None] * colpass[:, 0:out_rows]
    for a in range(1, tap_count):
        result = result + row_taps[:, a, None, None] * colpass[:, a:a + out_rows]
    return result.astype(jnp.bfloat16)

def matched_pair(science, inv_var, psf_rows, psf_cols, out_rows):
    science_f = science.astype(jnp.float32)
    inverse = inv_var.astype(jnp.float32)
    signal_map = filter_one(science_f * inverse, psf_rows, psf_cols, out_rows)
    depth_map = filter_one(inverse, psf_rows * psf_rows, psf_cols * psf_cols, out_rows)
    return (signal_map, depth_map)

def reference(science, inv_var, psf_rows, psf_cols, row_shift, col_shift, exposure_ok):
    radius = PSF_RAD

    def windows(signal_map, depth_map, shifts_row, shifts_col):
        stacked = jnp.stack([signal_map, depth_map])
        padded = jnp.pad(stacked, ((0, 0), (0, SHIFT), (SHIFT, SHIFT)))

        def cut_one(row_at, col_at):
            return lax.dynamic_slice(padded, (jnp.zeros((), jnp.int32), row_at.astype(jnp.int32), (col_at + SHIFT).astype(jnp.int32)), (2, ROWS, COLS))
        return jax.vmap(cut_one)(shifts_row, shifts_col).astype(jnp.float32)

    def shifted(scan_item):
        sci_one, inv_one, rows_one, cols_one, shifts_row, shifts_col, usable = scan_item
        sci_pad = jnp.pad(sci_one[None], ((0, 0), (radius, radius), (0, 0)))
        inv_pad = jnp.pad(inv_one[None], ((0, 0), (radius, radius), (0, 0)))
        signal_map, depth_map = matched_pair(sci_pad, inv_pad, rows_one[None], cols_one[None], ROWS)
        return (windows(signal_map[0], depth_map[0], shifts_row, shifts_col), usable.astype(jnp.float32))
    scan_items = (science, inv_var, psf_rows, psf_cols, row_shift, col_shift, exposure_ok)

    def first_step(running, scan_item):
        windows_now, usable = shifted(scan_item)
        return (running + usable * windows_now, None)
    zeros_init = jnp.zeros((VELS, 2, ROWS, COLS), jnp.float32)
    firsts, _ = lax.scan(first_step, zeros_init, scan_items)
    flux_est = firsts[:, 0] / (firsts[:, 1] + 1.0)

    def second_step(running, scan_item):
        windows_now, usable = shifted(scan_item)
        signal = windows_now[:, 0]
        depth = windows_now[:, 1]
        residual = signal - flux_est * depth
        weight = usable / (1.0 + residual * residual / (depth + 1.0))
        return (running + jnp.stack([weight * signal, weight * depth], 1), None)
    robust, _ = lax.scan(second_step, zeros_init, scan_items)
    likelihood = robust[:, 0] / jnp.sqrt(robust[:, 1] + 1.0)
    return likelihood.reshape(VELS, N_STRIP, ROWS_DEV, COLS).transpose(1, 0, 2, 3)
```

```python
import functools

import jax
import jax.numpy as jnp
from jax import lax
from jax.experimental import pallas as pl
from jax.experimental.pallas import tpu as pltpu

SHIFT = 16
LANES = 128
MESH = pl.DeviceIdType.MESH


def roll4(x):
    return pltpu.roll(x, 4, axis=x.ndim - 2)


def kernel(
    cfg,
    row_taps, col_taps, row_shift, col_shift, usable, sci, inv,
    out,
    above, below, rows_in, maps, fluxes, *rest,
):
    count, strips, exposures, rows, columns, vels, taps = cfg
    radius = taps // 2
    chips = count // 2
    own = rows // count
    half = rows // 2
    blocks = columns // LANES
    groups = vels // 2
    wide = columns + LANES
    map_rows = rows + SHIFT
    sums, near, pair, far = zip(rest[0:4], rest[4:8])
    (halo_s, halo_r, near_s, near_r, far_s, far_r, flux_s, flux_r, fsib_s, fsib_r) = rest[8:]

    me = lax.axis_index("expo")
    strip = lax.axis_index("strip")
    chip, core = me // 2, me % 2
    sibling = chip * 2 + (1 - core)
    has_above = strip > 0
    has_below = strip < strips - 1

    def peer(j):
        return (chip + j) % chips

    def halo_copy(e, array, down):
        source = (sci, inv)[array]
        if down:
            src, dst, to = source.at[e, pl.ds(rows - 16, 16)], above.at[array, e], strip + 1
        else:
            src, dst, to = source.at[e], below.at[array, e], strip - 1
        slot = (1 if down else 0, array, e)
        return pltpu.make_async_remote_copy(
            src_ref=src, dst_ref=dst, send_sem=halo_s.at[slot], recv_sem=halo_r.at[slot],
            device_id={"strip": to}, device_id_type=MESH,
        )

    def near_copy(stage, g):
        return pltpu.make_async_remote_copy(
            src_ref=sums[stage].at[g, 1 - core], dst_ref=near[stage].at[g],
            send_sem=near_s.at[stage, g], recv_sem=near_r.at[stage, g],
            device_id={"expo": sibling}, device_id_type=MESH,
        )

    def far_copy(stage, g, j):
        return pltpu.make_async_remote_copy(
            src_ref=pair[stage].at[g, peer(j)], dst_ref=far[stage].at[g, j - 1],
            send_sem=far_s.at[stage, g, j - 1], recv_sem=far_r.at[stage, g, j - 1],
            device_id={"expo": peer(j) * 2 + core}, device_id_type=MESH,
        )

    def flux_copy(g, j):
        mine = fluxes.at[g, core, chip]
        return pltpu.make_async_remote_copy(
            src_ref=mine, dst_ref=mine,
            send_sem=flux_s.at[g, j - 1], recv_sem=flux_r.at[g, j - 1],
            device_id={"expo": peer(j) * 2 + core}, device_id_type=MESH,
        )

    def flux_sibling(g):
        mine = fluxes.at[g, core]
        return pltpu.make_async_remote_copy(
            src_ref=mine, dst_ref=mine, send_sem=fsib_s.at[g], recv_sem=fsib_r.at[g],
            device_id={"expo": sibling}, device_id_type=MESH,
        )

    barrier = pltpu.get_barrier_semaphore()
    pl.semaphore_signal(barrier, inc=1, device_id={"expo": sibling}, device_id_type=MESH)
    for j in range(1, chips):
        pl.semaphore_signal(
            barrier, inc=1, device_id={"expo": peer(j) * 2 + core}, device_id_type=MESH
        )

    @pl.when(has_above)
    def _():
        pl.semaphore_signal(barrier, inc=1, device_id={"strip": strip - 1}, device_id_type=MESH)

    @pl.when(has_below)
    def _():
        pl.semaphore_signal(barrier, inc=1, device_id={"strip": strip + 1}, device_id_type=MESH)

    pl.semaphore_wait(barrier, chips + has_above.astype(jnp.int32) + has_below.astype(jnp.int32))

    @pl.when(has_above)
    def _():
        @pl.loop(0, exposures)
        def _(e):
            for array in (0, 1):
                halo_copy(e, array, False).start()

    @pl.when(has_below)
    def _():
        @pl.loop(0, exposures)
        def _(e):
            for array in (0, 1):
                halo_copy(e, array, True).start()

    @pl.when(jnp.logical_not(has_above))
    def _():
        above[...] = jnp.zeros_like(above)

    @pl.when(jnp.logical_not(has_below))
    def _():
        below[...] = jnp.zeros_like(below)

    lane = lax.broadcasted_iota(jnp.int32, (map_rows, wide), 1)
    row = lax.broadcasted_iota(jnp.int32, (map_rows, wide), 0)
    keep = (lane >= SHIFT) & (lane < SHIFT + columns) & ((row < rows) | has_below)

    flat = maps.reshape(4, exposures * rows * 8, LANES)

    @pl.loop(0, exposures)
    def _(e):
        @pl.when(has_below)
        def _():
            for array in (0, 1):
                halo_copy(e, array, False).wait_recv()

        @pl.when(has_above)
        def _():
            for array in (0, 1):
                halo_copy(e, array, True).wait_recv()

        for place, size, pick in (
            (0, 16, lambda k: above[k, e]),
            (16, rows, lambda k: (sci, inv)[k][e]),
            (16 + rows, rows, lambda k: below[k, e]),
        ):
            inverse = pick(1).astype(jnp.float32)
            rows_in[0, pl.ds(place, size), :] = pick(0).astype(jnp.float32) * inverse
            rows_in[1, pl.ds(place, size), :] = inverse
        ok = usable[e].astype(jnp.float32)
        for which in (0, 1):
            def tap(ref, a):
                value = ref[e, a]
                return value * value if which else value

            filtered = tap(row_taps, 0) * rows_in[which, pl.ds(16 - radius, map_rows), :]
            for a in range(1, taps):
                filtered += tap(row_taps, a) * rows_in[which, pl.ds(16 - radius + a, map_rows), :]
            filtered = jnp.concatenate(
                [filtered, jnp.zeros((map_rows, LANES), jnp.float32)], axis=1
            )
            result = tap(col_taps, 0) * pltpu.roll(filtered, SHIFT + radius, axis=1)
            for b in range(1, taps):
                result += tap(col_taps, b) * pltpu.roll(filtered, SHIFT + radius - b, axis=1)
            result = jnp.where(keep, result, 0.0).astype(jnp.bfloat16).astype(jnp.float32) * ok
            for block in range(blocks + 1):
                for r in range(0, map_rows, 8):
                    tile = result[r : r + 8, block * LANES : (block + 1) * LANES]
                    for later in (0, 1):
                        sub = block - later
                        if sub < 0 or sub >= blocks:
                            continue
                        for at, shift in ((r, sub), (r - half, sub + 4)):
                            if 0 <= at < rows:
                                flat[2 * which + later,
                                     pl.ds((e * rows + at) * 8 + shift, 8, stride=8), :] = tile

    low = lax.broadcasted_iota(jnp.int32, (1, 8, LANES), 1) < 4
    lane8 = lax.broadcasted_iota(jnp.int32, (1, 8, LANES), 2)

    def window(e, velocity, which, start):
        at = e * rows + row_shift[e, velocity] + start
        shift = col_shift[e, velocity] + SHIFT
        here = maps[2 * which, pl.ds(at, 8)]
        after = maps[2 * which + 1, pl.ds(at, 8)]
        mixed = jnp.where(jnp.broadcast_to(lane8 >= shift, here.shape), here, after)
        return pltpu.roll(mixed, LANES - shift, axis=2)

    def put(stage, g, v, start, signal, depth):
        for base, value in (
            (start, jnp.where(low, signal, roll4(depth))),
            (start + half, jnp.where(low, roll4(signal), depth)),
        ):
            for part in range(8 // own):
                owner = base // own + part
                sums[stage][g, owner % 2, owner // 2, v] = value[part * own : (part + 1) * own]

    def get_rows(g, start):
        return jnp.concatenate(
            [
                fluxes[g, (start // own + part) % 2, (start // own + part) // 2]
                for part in range(8 // own)
            ],
            axis=0,
        )

    def pass_on(stage, g):
        near_copy(stage, g).wait_recv()
        pair[stage][g] = sums[stage][g, core] + near[stage][g]
        for j in range(1, chips):
            far_copy(stage, g, j).start()

    def total(stage, g):
        value = pair[stage][g, chip]
        for j in range(1, chips):
            far_copy(stage, g, j).wait_recv()
            value = value + far[stage][g, j - 1]
        return value

    @pl.loop(0, groups)
    def _(g):
        for v in (0, 1):
            for start in range(0, half, 8):
                signal = window(0, 2 * g + v, 0, start)
                depth = window(0, 2 * g + v, 1, start)
                for e in range(1, exposures):
                    signal += window(e, 2 * g + v, 0, start)
                    depth += window(e, 2 * g + v, 1, start)
                put(0, g, v, start, signal, depth)
        near_copy(0, g).start()

        @pl.when(g > 0)
        def _():
            pass_on(0, g - 1)

    pass_on(0, groups - 1)

    @pl.loop(0, groups)
    def _(g):
        whole = total(0, g)
        flux = whole / (roll4(whole) + 1.0)
        fluxes[g, core, chip] = jnp.where(low, flux[0], roll4(flux[1]))
        for j in range(1, chips):
            flux_copy(g, j).start()

        @pl.when(g > 0)
        def _():
            for j in range(1, chips):
                flux_copy(g - 1, j).wait_recv()
            flux_sibling(g - 1).start()

    for j in range(1, chips):
        flux_copy(groups - 1, j).wait_recv()
    flux_sibling(groups - 1).start()

    @pl.loop(0, groups)
    def _(g):
        flux_sibling(g).wait_recv()
        for v in (0, 1):
            for start in range(0, half, 8):
                upper, lower = get_rows(g, start), get_rows(g, start + half)
                if v == 0:
                    flux = jnp.where(low, upper, roll4(lower))
                else:
                    flux = jnp.where(low, roll4(upper), lower)
                signal_sum = jnp.zeros((8, 8, LANES), jnp.float32)
                depth_sum = jnp.zeros((8, 8, LANES), jnp.float32)
                for e in range(exposures):
                    signal = window(e, 2 * g + v, 0, start)
                    depth = window(e, 2 * g + v, 1, start)
                    residual = signal - flux * depth
                    more = depth + 1.0
                    weight = more / (more + residual * residual)
                    signal_sum += weight * signal
                    depth_sum += weight * depth
                put(1, g, v, start, signal_sum, depth_sum)
        near_copy(1, g).start()

        @pl.when(g > 0)
        def _():
            pass_on(1, g - 1)

    pass_on(1, groups - 1)

    @pl.loop(0, groups)
    def _(g):
        whole = total(1, g)
        result = whole / jnp.sqrt(roll4(whole) + 1.0)
        for v in (0, 1):
            out[2 * g + v] = result[v, :, :4, :]

    @pl.loop(0, groups)
    def _(g):
        for stage in (0, 1):
            near_copy(stage, g).wait_send()
            for j in range(1, chips):
                far_copy(stage, g, j).wait_send()
        for j in range(1, chips):
            flux_copy(g, j).wait_send()
        flux_sibling(g).wait_send()

    @pl.when(has_above)
    def _():
        @pl.loop(0, exposures)
        def _(e):
            for array in (0, 1):
                halo_copy(e, array, False).wait_send()

    @pl.when(has_below)
    def _():
        @pl.loop(0, exposures)
        def _(e):
            for array in (0, 1):
                halo_copy(e, array, True).wait_send()


def per_device(count, strips, science, inv_var, psf_rows, psf_cols, row_shift, col_shift, ok):
    exposures, rows, columns = science.shape
    vels, taps = row_shift.shape[1], psf_rows.shape[1]
    chips, own, groups = count // 2, rows // count, vels // 2
    f32, bf16 = jnp.float32, jnp.bfloat16
    dma = lambda *shape: [pltpu.SemaphoreType.DMA(shape)] * 2
    smem = pl.BlockSpec(memory_space=pltpu.SMEM)
    vmem = pl.BlockSpec(memory_space=pltpu.VMEM)
    result = pl.pallas_call(
        functools.partial(kernel, (count, strips, exposures, rows, columns, vels, taps)),
        out_shape=jax.ShapeDtypeStruct((vels, own, columns // LANES, LANES), f32),
        in_specs=[smem] * 5 + [vmem] * 2,
        out_specs=vmem,
        scratch_shapes=[
            pltpu.VMEM((2, exposures, 16, columns), bf16),
            pltpu.VMEM((2, exposures, rows, columns), bf16),
            pltpu.VMEM((2, 16 + 2 * rows, columns), f32),
            pltpu.VMEM((4, exposures * rows, 8, LANES), f32),
            pltpu.VMEM((groups, 2, chips, own, 8, LANES), f32),
            pltpu.VMEM((groups, 2, chips, 2, own, 8, LANES), f32),
            pltpu.VMEM((groups, chips, 2, own, 8, LANES), f32),
            pltpu.VMEM((groups, chips, 2, own, 8, LANES), f32),
            pltpu.VMEM((groups, chips - 1, 2, own, 8, LANES), f32),
            pltpu.VMEM((groups, 2, chips, 2, own, 8, LANES), f32),
            pltpu.VMEM((groups, chips, 2, own, 8, LANES), f32),
            pltpu.VMEM((groups, chips, 2, own, 8, LANES), f32),
            pltpu.VMEM((groups, chips - 1, 2, own, 8, LANES), f32),
            *dma(2, 2, exposures),
            *dma(2, groups),
            *dma(2, groups, chips - 1),
            *dma(groups, chips - 1),
            *dma(groups),
        ],
        compiler_params=pltpu.CompilerParams(
            collective_id=0, has_side_effects=True, vmem_limit_bytes=40 * 1024 * 1024
        ),
    )(psf_rows, psf_cols, row_shift, col_shift, ok, science, inv_var)
    return result.reshape(1, vels, own, columns)


def solution(mesh):
    from jax.sharding import PartitionSpec as P

    in_specs = (
        P(("field", "expo"), "strip", None),
        P(("field", "expo"), "strip", None),
        P(("field", "expo"), None),
        P(("field", "expo"), None),
        P(("field", "expo"), None),
        P(("field", "expo"), None),
        P(("field", "expo")),
    )
    return jax.shard_map(
        functools.partial(per_device, mesh.shape["expo"], mesh.shape["strip"]),
        mesh=mesh,
        in_specs=in_specs,
        out_specs=P("strip", "field", "expo", None),
        check_vma=False,
    )
```

```python
import functools

import jax
import jax.numpy as jnp
from jax import lax
from jax.experimental import pallas as pl
from jax.experimental.pallas import tpu as pltpu

SHIFT = 16
LANES = 128
MESH = pl.DeviceIdType.MESH


def roll4(x):
    return pltpu.roll(x, 4, axis=x.ndim - 2)


def kernel(
    cfg,
    *refs,
):
    out, inputs, copied = refs[7], refs[:7], refs[8:15]
    row_taps, col_taps, row_shift, col_shift, usable, sci, inv = copied
    (in_s, below, tails, above, edge_out, edges, rows_in, maps, stacks, fluxes, *rest) = refs[15:]
    count, strips, exposures, rows, columns, vels, taps = cfg
    radius = taps // 2
    chips = count // 2
    own = rows // count
    half = rows // 2
    blocks = columns // LANES
    groups = vels // 2
    wide = columns + LANES
    map_rows = rows + SHIFT
    sums, near, mine, pair, far = zip(rest[0:5], rest[5:10])
    (full_s, full_r, edge_s, edge_r, near_s, near_r,
     far_s, far_r, flux_s, flux_r, fsib_s, fsib_r) = rest[10:]
    per_tile = 16 // radius
    tiles = exposures // per_tile

    me = lax.axis_index("expo")
    strip = lax.axis_index("strip")
    chip, core = me // 2, me % 2
    sibling = chip * 2 + (1 - core)
    has_above = strip > 0
    has_below = strip < strips - 1

    def peer(j):
        return (chip + j) % chips

    def full_copy(e, array):
        return pltpu.make_async_remote_copy(
            src_ref=(sci, inv)[array].at[e, pl.ds(0, SHIFT)], dst_ref=below.at[array, e],
            send_sem=full_s.at[array, e], recv_sem=full_r.at[array, e],
            device_id={"strip": strip - 1}, device_id_type=MESH,
        )

    def edge_copy(t, array, down):
        return pltpu.make_async_remote_copy(
            src_ref=edge_out.at[down, array, t], dst_ref=(tails, above)[down].at[array, t],
            send_sem=edge_s.at[down, array, t], recv_sem=edge_r.at[down, array, t],
            device_id={"strip": strip + 1 if down else strip - 1}, device_id_type=MESH,
        )

    def near_copy(stage, g):
        return pltpu.make_async_remote_copy(
            src_ref=sums[stage].at[g, 1 - core], dst_ref=near[stage].at[g],
            send_sem=near_s.at[stage, g], recv_sem=near_r.at[stage, g],
            device_id={"expo": sibling}, device_id_type=MESH,
        )

    def far_copy(stage, g, j):
        return pltpu.make_async_remote_copy(
            src_ref=pair[stage].at[g, peer(j)], dst_ref=far[stage].at[g, j - 1],
            send_sem=far_s.at[stage, g, j - 1], recv_sem=far_r.at[stage, g, j - 1],
            device_id={"expo": peer(j) * 2 + core}, device_id_type=MESH,
        )

    def flux_copy(g, j):
        mine = fluxes.at[g, core, chip]
        return pltpu.make_async_remote_copy(
            src_ref=mine, dst_ref=mine,
            send_sem=flux_s.at[g, j - 1], recv_sem=flux_r.at[g, j - 1],
            device_id={"expo": peer(j) * 2 + core}, device_id_type=MESH,
        )

    def flux_sibling(g):
        mine = fluxes.at[g, core]
        return pltpu.make_async_remote_copy(
            src_ref=mine, dst_ref=mine, send_sem=fsib_s.at[g], recv_sem=fsib_r.at[g],
            device_id={"expo": sibling}, device_id_type=MESH,
        )

    local = [
        pltpu.make_async_copy(inputs[k], copied[k], in_s.at[k]) for k in (5, 6, 0, 1, 2, 3, 4)
    ]
    for copy in local:
        copy.start()
    barrier = pltpu.get_barrier_semaphore()
    pl.semaphore_signal(barrier, inc=1, device_id={"expo": sibling}, device_id_type=MESH)
    for j in range(1, chips):
        pl.semaphore_signal(
            barrier, inc=1, device_id={"expo": peer(j) * 2 + core}, device_id_type=MESH
        )

    @pl.when(has_above)
    def _():
        pl.semaphore_signal(barrier, inc=1, device_id={"strip": strip - 1}, device_id_type=MESH)

    @pl.when(has_below)
    def _():
        pl.semaphore_signal(barrier, inc=1, device_id={"strip": strip + 1}, device_id_type=MESH)

    for copy in local[:2]:
        copy.wait()
    for array, source in enumerate((sci, inv)):
        for t in range(tiles):
            span = range(t * per_tile, (t + 1) * per_tile)
            for down, at in ((0, SHIFT), (1, rows - radius)):
                base = at // 16 * 16
                pieces = [
                    source[e, base : base + 16, :].astype(jnp.float32)[
                        at - base : at - base + radius
                    ]
                    for e in span
                ]
                edge_out[down, array, t] = jnp.concatenate(pieces, axis=0).astype(jnp.bfloat16)
    pl.semaphore_wait(barrier, chips + has_above.astype(jnp.int32) + has_below.astype(jnp.int32))

    @pl.when(has_below)
    def _():
        for t in range(tiles):
            for array in (0, 1):
                edge_copy(t, array, 1).start()

    @pl.when(has_above)
    def _():
        @pl.loop(0, tiles)
        def _(t):
            for array in (0, 1):
                edge_copy(t, array, 0).start()

            @pl.loop(0, per_tile)
            def _(q):
                for array in (0, 1):
                    full_copy(t * per_tile + q, array).start()

    @pl.when(jnp.logical_not(has_above))
    def _():
        above[...] = jnp.zeros_like(above)

    @pl.when(jnp.logical_not(has_below))
    def _():
        below[...] = jnp.zeros_like(below)
        tails[...] = jnp.zeros_like(tails)

    stacks[...] = jnp.zeros_like(stacks)
    for copy in local[2:]:
        copy.wait()

    lane = lax.broadcasted_iota(jnp.int32, (map_rows, wide), 1)
    row = lax.broadcasted_iota(jnp.int32, (map_rows, wide), 0)
    keep = (lane >= SHIFT) & (lane < SHIFT + columns) & ((row < rows) | has_below)

    low = lax.broadcasted_iota(jnp.int32, (1, 8, LANES), 1) < 4
    lane8 = lax.broadcasted_iota(jnp.int32, (1, 8, LANES), 2)

    def window(e, velocity, which, start):
        at = e * rows + row_shift[e, velocity] + start
        shift = col_shift[e, velocity] + SHIFT
        here = maps[2 * which, pl.ds(at, 8)]
        after = maps[2 * which + 1, pl.ds(at, 8)]
        mixed = jnp.where(jnp.broadcast_to(lane8 >= shift, here.shape), here, after)
        return pltpu.roll(mixed, (LANES - shift) & (LANES - 1), axis=2)

    flat = maps.reshape(4, exposures * rows * 8, LANES)

    @pl.loop(0, exposures)
    def _(e):
        tile_now, place_in_tile = e // per_tile, e % per_tile

        @pl.when(place_in_tile == 0)
        def _():
            @pl.when(has_below)
            def _():
                for array in (0, 1):
                    edge_copy(tile_now, array, 0).wait_recv()

            @pl.when(has_above)
            def _():
                for array in (0, 1):
                    edge_copy(tile_now, array, 1).wait_recv()

            for down, source in enumerate((tails, above)):
                for array in (0, 1):
                    tile = source[array, tile_now].astype(jnp.float32)
                    for q in range(per_tile):
                        piece = tile[q * radius : (q + 1) * radius]
                        edges[down, array, q] = jnp.concatenate([piece] * (8 // radius), axis=0)

        @pl.when(has_below)
        def _():
            for array in (0, 1):
                full_copy(e, array).wait_recv()

        for place, size, pick in (
            (0, 8, lambda k: edges[1, k, place_in_tile]),
            (8, rows, lambda k: (sci, inv)[k][e]),
            (8 + rows, SHIFT, lambda k: below[k, e]),
            (8 + rows + SHIFT, 8, lambda k: edges[0, k, place_in_tile]),
        ):
            inverse = pick(1).astype(jnp.float32)
            rows_in[0, pl.ds(place, size), :] = pick(0).astype(jnp.float32) * inverse
            rows_in[1, pl.ds(place, size), :] = inverse
        ok = usable[e].astype(jnp.float32)
        for which in (0, 1):
            def tap(ref, a):
                value = ref[e, a]
                return value * value if which else value

            filtered = tap(row_taps, 0) * rows_in[which, pl.ds(8 - radius, map_rows), :]
            for a in range(1, taps):
                filtered += tap(row_taps, a) * rows_in[which, pl.ds(8 - radius + a, map_rows), :]
            filtered = jnp.concatenate(
                [filtered, jnp.zeros((map_rows, LANES), jnp.float32)], axis=1
            )
            result = tap(col_taps, 0) * pltpu.roll(filtered, SHIFT + radius, axis=1)
            for b in range(1, taps):
                result += tap(col_taps, b) * pltpu.roll(filtered, SHIFT + radius - b, axis=1)
            result = jnp.where(keep, result, 0.0).astype(jnp.bfloat16).astype(jnp.float32) * ok
            for block in range(blocks + 1):
                for r in range(0, map_rows, 8):
                    tile = result[r : r + 8, block * LANES : (block + 1) * LANES]
                    for later in (0, 1):
                        sub = block - later
                        if sub < 0 or sub >= blocks:
                            continue
                        for at, shift in ((r, sub), (r - half, sub + 4)):
                            if 0 <= at < rows:
                                flat[2 * which + later,
                                     pl.ds((e * rows + at) * 8 + shift, 8, stride=8), :] = tile

        @pl.loop(0, vels)
        def _(velocity):
            for which in (0, 1):
                for start in range(0, half, 8):
                    stacks[velocity, which, pl.ds(start, 8)] += window(e, velocity, which, start)

    def put(stage, g, v, start, signal, depth):
        for base, value in (
            (start, jnp.where(low, signal, roll4(depth))),
            (start + half, jnp.where(low, roll4(signal), depth)),
        ):
            for part in range(8 // own):
                owner = base // own + part
                sums[stage][g, owner % 2, owner // 2, v] = value[part * own : (part + 1) * own]

    def get_rows(g, start):
        return jnp.concatenate(
            [
                fluxes[g, (start // own + part) % 2, (start // own + part) // 2]
                for part in range(8 // own)
            ],
            axis=0,
        )

    def pass_on(stage, g):
        near_copy(stage, g).wait_recv()
        mine[stage][g] = sums[stage][g, core, chip] + near[stage][g, chip]
        for j in range(1, chips):
            there = peer(j)
            both = sums[stage][g, core, there] + near[stage][g, there]
            pair[stage][g, there] = both.reshape(2, own * 8, LANES).astype(jnp.bfloat16)
            far_copy(stage, g, j).start()

    def total(stage, g):
        value = mine[stage][g]
        for j in range(1, chips):
            far_copy(stage, g, j).wait_recv()
            value = value + far[stage][g, j - 1].astype(jnp.float32).reshape(value.shape)
        return value

    @pl.loop(0, groups)
    def _(g):
        for v in (0, 1):
            for start in range(0, half, 8):
                put(
                    0, g, v, start,
                    stacks[2 * g + v, 0, pl.ds(start, 8)], stacks[2 * g + v, 1, pl.ds(start, 8)],
                )
        near_copy(0, g).start()

        @pl.when(g > 0)
        def _():
            pass_on(0, g - 1)

    pass_on(0, groups - 1)

    @pl.loop(0, groups)
    def _(g):
        whole = total(0, g)
        flux = whole / (roll4(whole) + 1.0)
        fluxes[g, core, chip] = jnp.where(low, flux[0], roll4(flux[1]))
        for j in range(1, chips):
            flux_copy(g, j).start()

        @pl.when(g > 0)
        def _():
            for j in range(1, chips):
                flux_copy(g - 1, j).wait_recv()
            flux_sibling(g - 1).start()

    for j in range(1, chips):
        flux_copy(groups - 1, j).wait_recv()
    flux_sibling(groups - 1).start()

    @pl.loop(0, groups)
    def _(g):
        flux_sibling(g).wait_recv()
        for v in (0, 1):
            for start in range(0, half, 8):
                upper, lower = get_rows(g, start), get_rows(g, start + half)
                if v == 0:
                    flux = jnp.where(low, upper, roll4(lower))
                else:
                    flux = jnp.where(low, roll4(upper), lower)
                signal_sum = jnp.zeros((8, 8, LANES), jnp.float32)
                depth_sum = jnp.zeros((8, 8, LANES), jnp.float32)
                for e in range(exposures):
                    signal = window(e, 2 * g + v, 0, start)
                    depth = window(e, 2 * g + v, 1, start)
                    residual = signal - flux * depth
                    more = depth + 1.0
                    weight = more / (more + residual * residual)
                    signal_sum += weight * signal
                    depth_sum += weight * depth
                put(1, g, v, start, signal_sum, depth_sum)
        near_copy(1, g).start()

        @pl.when(g > 0)
        def _():
            pass_on(1, g - 1)

    pass_on(1, groups - 1)

    @pl.loop(0, groups)
    def _(g):
        whole = total(1, g)
        result = whole / jnp.sqrt(roll4(whole) + 1.0)
        for v in (0, 1):
            out[2 * g + v] = result[v, :, :4, :]

    @pl.loop(0, groups)
    def _(g):
        for stage in (0, 1):
            near_copy(stage, g).wait_send()
            for j in range(1, chips):
                far_copy(stage, g, j).wait_send()
        for j in range(1, chips):
            flux_copy(g, j).wait_send()
        flux_sibling(g).wait_send()

    @pl.when(has_below)
    def _():
        for t in range(tiles):
            for array in (0, 1):
                edge_copy(t, array, 1).wait_send()

    @pl.when(has_above)
    def _():
        for t in range(tiles):
            for array in (0, 1):
                edge_copy(t, array, 0).wait_send()

        @pl.loop(0, exposures)
        def _(e):
            for array in (0, 1):
                full_copy(e, array).wait_send()


def per_device(count, strips, science, inv_var, psf_rows, psf_cols, row_shift, col_shift, ok):
    exposures, rows, columns = science.shape
    vels, taps = row_shift.shape[1], psf_rows.shape[1]
    chips, own, groups = count // 2, rows // count, vels // 2
    f32, bf16 = jnp.float32, jnp.bfloat16
    dma = lambda *shape: [pltpu.SemaphoreType.DMA(shape)] * 2
    radius = taps // 2
    tiles = exposures * radius // 16
    stage = [
        pltpu.VMEM((groups, 2, chips, 2, own, 8, LANES), f32),
        pltpu.VMEM((groups, chips, 2, own, 8, LANES), f32),
        pltpu.VMEM((groups, 2, own, 8, LANES), f32),
        pltpu.VMEM((groups, chips, 2, own * 8, LANES), bf16),
        pltpu.VMEM((groups, chips - 1, 2, own * 8, LANES), bf16),
    ]
    result = pl.pallas_call(
        functools.partial(kernel, (count, strips, exposures, rows, columns, vels, taps)),
        out_shape=jax.ShapeDtypeStruct((vels, own, columns // LANES, LANES), f32),
        in_specs=[pl.BlockSpec(memory_space=pl.ANY)] * 7,
        out_specs=pl.BlockSpec(memory_space=pltpu.VMEM),
        scratch_shapes=[
            pltpu.SMEM(psf_rows.shape, f32),
            pltpu.SMEM(psf_cols.shape, f32),
            pltpu.SMEM(row_shift.shape, jnp.int32),
            pltpu.SMEM(col_shift.shape, jnp.int32),
            pltpu.SMEM(ok.shape, jnp.int32),
            pltpu.VMEM(science.shape, bf16),
            pltpu.VMEM(science.shape, bf16),
            pltpu.SemaphoreType.DMA((7,)),
            pltpu.VMEM((2, exposures, SHIFT, columns), bf16),
            pltpu.VMEM((2, tiles, 16, columns), bf16),
            pltpu.VMEM((2, tiles, 16, columns), bf16),
            pltpu.VMEM((2, 2, tiles, 16, columns), bf16),
            pltpu.VMEM((2, 2, 16 // radius, 8, columns), f32),
            pltpu.VMEM((2, 16 + rows + SHIFT, columns), f32),
            pltpu.VMEM((4, exposures * rows, 8, LANES), f32),
            pltpu.VMEM((vels, 2, rows // 2, 8, LANES), f32),
            pltpu.VMEM((groups, 2, chips, own, 8, LANES), f32),
            *stage,
            *stage,
            *dma(2, exposures),
            *dma(2, 2, tiles),
            *dma(2, groups),
            *dma(2, groups, chips - 1),
            *dma(groups, chips - 1),
            *dma(groups),
        ],
        compiler_params=pltpu.CompilerParams(
            collective_id=0, has_side_effects=True, vmem_limit_bytes=60 * 1024 * 1024
        ),
    )(psf_rows, psf_cols, row_shift, col_shift, ok, science, inv_var)
    return result.reshape(1, vels, own, columns)


def solution(mesh):
    from jax.sharding import PartitionSpec as P

    in_specs = (
        P(("field", "expo"), "strip", None),
        P(("field", "expo"), "strip", None),
        P(("field", "expo"), None),
        P(("field", "expo"), None),
        P(("field", "expo"), None),
        P(("field", "expo"), None),
        P(("field", "expo")),
    )
    return jax.shard_map(
        functools.partial(per_device, mesh.shape["expo"], mesh.shape["strip"]),
        mesh=mesh,
        in_specs=in_specs,
        out_specs=P("strip", "field", "expo", None),
        check_vma=False,
    )
```

```python
import functools
import math

import jax
import jax.numpy as jnp
from jax import lax
from jax.experimental import pallas as pl
from jax.experimental.pallas import tpu as pltpu

SHIFT = 16
LANES = 128
MESH = pl.DeviceIdType.MESH


LEAST = 2.0 ** -20
STEPS = 32700.0


def to_code(x, steps):
    level = jnp.log(1.0 + jnp.abs(x) * (1.0 / LEAST)) * steps + 0.5
    return jnp.where(x < 0, -level, level).astype(jnp.int32).astype(jnp.int16)


def from_code(code, steps):
    level = code.astype(jnp.int32).astype(jnp.float32)
    size = (jnp.exp(jnp.abs(level) * (1.0 / steps)) - 1.0) * LEAST
    return jnp.where(level < 0, -size, size)


def roll4(x):
    return pltpu.roll(x, 4, axis=x.ndim - 2)


def kernel(
    cfg,
    *refs,
):
    out, inputs, copied = refs[7], refs[:7], refs[8:15]
    row_taps, col_taps, row_shift, col_shift, usable, sci, inv = copied
    (in_s, below, tails, above, edge_out, edges, rows_in, maps, stacks, fluxes, final, *rest) = refs[15:]
    count, strips, exposures, rows, columns, vels, taps = cfg
    radius = taps // 2
    chips = count // 2
    own = rows // count
    half = rows // 2
    blocks = columns // LANES
    groups = vels // 2
    wide = columns + LANES
    map_rows = rows + SHIFT
    sums, near, mine, pair, far = zip(rest[0:5], rest[5:10])
    (full_s, full_r, edge_s, edge_r, near_s, near_r,
     far_s, far_r, flux_s, flux_r, fsib_s, fsib_r) = rest[10:]
    per_tile = 16 // radius
    most = 2.0 * exposures * 24.0 * taps * taps * 1.01
    steps = STEPS / math.log(1.0 + most / LEAST)
    tiles = exposures // per_tile

    me = lax.axis_index("expo")
    strip = lax.axis_index("strip")
    chip, core = me // 2, me % 2
    sibling = chip * 2 + (1 - core)
    has_above = strip > 0
    has_below = strip < strips - 1

    def peer(j):
        return (chip + j) % chips

    def full_copy(e, array):
        return pltpu.make_async_remote_copy(
            src_ref=(sci, inv)[array].at[e, pl.ds(0, SHIFT)], dst_ref=below.at[array, e],
            send_sem=full_s.at[array, e], recv_sem=full_r.at[array, e],
            device_id={"strip": strip - 1}, device_id_type=MESH,
        )

    def edge_copy(t, array, down):
        return pltpu.make_async_remote_copy(
            src_ref=edge_out.at[down, array, t], dst_ref=(tails, above)[down].at[array, t],
            send_sem=edge_s.at[down, array, t], recv_sem=edge_r.at[down, array, t],
            device_id={"strip": strip + 1 if down else strip - 1}, device_id_type=MESH,
        )

    def near_copy(stage, g):
        return pltpu.make_async_remote_copy(
            src_ref=sums[stage].at[g, 1 - core], dst_ref=near[stage].at[g],
            send_sem=near_s.at[stage, g], recv_sem=near_r.at[stage, g],
            device_id={"expo": sibling}, device_id_type=MESH,
        )

    def far_copy(stage, g, j):
        return pltpu.make_async_remote_copy(
            src_ref=pair[stage].at[g, peer(j)], dst_ref=far[stage].at[g, j - 1],
            send_sem=far_s.at[stage, g, j - 1], recv_sem=far_r.at[stage, g, j - 1],
            device_id={"expo": peer(j) * 2 + core}, device_id_type=MESH,
        )

    def flux_copy(g, j):
        mine = fluxes.at[g, core, chip]
        return pltpu.make_async_remote_copy(
            src_ref=mine, dst_ref=mine,
            send_sem=flux_s.at[g, j - 1], recv_sem=flux_r.at[g, j - 1],
            device_id={"expo": peer(j) * 2 + core}, device_id_type=MESH,
        )

    def flux_sibling(g):
        mine = fluxes.at[g, core]
        return pltpu.make_async_remote_copy(
            src_ref=mine, dst_ref=mine, send_sem=fsib_s.at[g], recv_sem=fsib_r.at[g],
            device_id={"expo": sibling}, device_id_type=MESH,
        )

    local = [
        pltpu.make_async_copy(inputs[k], copied[k], in_s.at[k]) for k in (5, 6, 0, 1, 2, 3, 4)
    ]
    for copy in local:
        copy.start()
    barrier = pltpu.get_barrier_semaphore()
    pl.semaphore_signal(barrier, inc=1, device_id={"expo": sibling}, device_id_type=MESH)
    for j in range(1, chips):
        pl.semaphore_signal(
            barrier, inc=1, device_id={"expo": peer(j) * 2 + core}, device_id_type=MESH
        )

    @pl.when(has_above)
    def _():
        pl.semaphore_signal(barrier, inc=1, device_id={"strip": strip - 1}, device_id_type=MESH)

    @pl.when(has_below)
    def _():
        pl.semaphore_signal(barrier, inc=1, device_id={"strip": strip + 1}, device_id_type=MESH)

    for copy in local[:2]:
        copy.wait()
    for array, source in enumerate((sci, inv)):
        for t in range(tiles):
            span = range(t * per_tile, (t + 1) * per_tile)
            for down, at in ((0, SHIFT), (1, rows - radius)):
                base = at // 16 * 16
                pieces = [
                    source[e, base : base + 16, :].astype(jnp.float32)[
                        at - base : at - base + radius
                    ]
                    for e in span
                ]
                edge_out[down, array, t] = jnp.concatenate(pieces, axis=0).astype(jnp.bfloat16)
    pl.semaphore_wait(barrier, chips + has_above.astype(jnp.int32) + has_below.astype(jnp.int32))

    @pl.when(has_below)
    def _():
        for t in range(tiles):
            for array in (0, 1):
                edge_copy(t, array, 1).start()

    @pl.when(has_above)
    def _():
        @pl.loop(0, tiles)
        def _(t):
            for array in (0, 1):
                edge_copy(t, array, 0).start()

            @pl.loop(0, per_tile)
            def _(q):
                for array in (0, 1):
                    full_copy(t * per_tile + q, array).start()

    @pl.when(jnp.logical_not(has_above))
    def _():
        above[...] = jnp.zeros_like(above)

    @pl.when(jnp.logical_not(has_below))
    def _():
        below[...] = jnp.zeros_like(below)
        tails[...] = jnp.zeros_like(tails)

    stacks[...] = jnp.zeros_like(stacks)
    for copy in local[2:]:
        copy.wait()

    lane = lax.broadcasted_iota(jnp.int32, (map_rows, wide), 1)
    row = lax.broadcasted_iota(jnp.int32, (map_rows, wide), 0)
    keep = (lane >= SHIFT) & (lane < SHIFT + columns) & ((row < rows) | has_below)

    low = lax.broadcasted_iota(jnp.int32, (1, 8, LANES), 1) < 4
    lane8 = lax.broadcasted_iota(jnp.int32, (1, 8, LANES), 2)

    def window(e, velocity, which, start):
        at = e * rows + row_shift[e, velocity] + start
        shift = col_shift[e, velocity] + SHIFT
        here = maps[2 * which, pl.ds(at, 8)]
        after = maps[2 * which + 1, pl.ds(at, 8)]
        mixed = jnp.where(jnp.broadcast_to(lane8 >= shift, here.shape), here, after)
        return pltpu.roll(mixed, (LANES - shift) & (LANES - 1), axis=2)

    flat = maps.reshape(4, exposures * rows * 8, LANES)

    @pl.loop(0, exposures)
    def _(e):
        tile_now, place_in_tile = e // per_tile, e % per_tile

        @pl.when(place_in_tile == 0)
        def _():
            @pl.when(has_below)
            def _():
                for array in (0, 1):
                    edge_copy(tile_now, array, 0).wait_recv()

            @pl.when(has_above)
            def _():
                for array in (0, 1):
                    edge_copy(tile_now, array, 1).wait_recv()

            for down, source in enumerate((tails, above)):
                for array in (0, 1):
                    tile = source[array, tile_now].astype(jnp.float32)
                    for q in range(per_tile):
                        piece = tile[q * radius : (q + 1) * radius]
                        edges[down, array, q] = jnp.concatenate([piece] * (8 // radius), axis=0)

        @pl.when(has_below)
        def _():
            for array in (0, 1):
                full_copy(e, array).wait_recv()

        for place, size, pick in (
            (0, 8, lambda k: edges[1, k, place_in_tile]),
            (8, rows, lambda k: (sci, inv)[k][e]),
            (8 + rows, SHIFT, lambda k: below[k, e]),
            (8 + rows + SHIFT, 8, lambda k: edges[0, k, place_in_tile]),
        ):
            inverse = pick(1).astype(jnp.float32)
            rows_in[0, pl.ds(place, size), :] = pick(0).astype(jnp.float32) * inverse
            rows_in[1, pl.ds(place, size), :] = inverse
        ok = usable[e].astype(jnp.float32)
        for which in (0, 1):
            def tap(ref, a):
                value = ref[e, a]
                return value * value if which else value

            filtered = tap(row_taps, 0) * rows_in[which, pl.ds(8 - radius, map_rows), :]
            for a in range(1, taps):
                filtered += tap(row_taps, a) * rows_in[which, pl.ds(8 - radius + a, map_rows), :]
            filtered = jnp.concatenate(
                [filtered, jnp.zeros((map_rows, LANES), jnp.float32)], axis=1
            )
            result = tap(col_taps, 0) * pltpu.roll(filtered, SHIFT + radius, axis=1)
            for b in range(1, taps):
                result += tap(col_taps, b) * pltpu.roll(filtered, SHIFT + radius - b, axis=1)
            result = jnp.where(keep, result, 0.0).astype(jnp.bfloat16).astype(jnp.float32) * ok
            for block in range(blocks + 1):
                for r in range(0, map_rows, 8):
                    tile = result[r : r + 8, block * LANES : (block + 1) * LANES]
                    for later in (0, 1):
                        sub = block - later
                        if sub < 0 or sub >= blocks:
                            continue
                        for at, shift in ((r, sub), (r - half, sub + 4)):
                            if 0 <= at < rows:
                                flat[2 * which + later,
                                     pl.ds((e * rows + at) * 8 + shift, 8, stride=8), :] = tile

        @pl.loop(0, vels)
        def _(velocity):
            for which in (0, 1):
                for start in range(0, half, 8):
                    stacks[velocity, which, pl.ds(start, 8)] += window(e, velocity, which, start)

    def put(stage, g, v, start, signal, depth):
        for base, value in (
            (start, jnp.where(low, signal, roll4(depth))),
            (start + half, jnp.where(low, roll4(signal), depth)),
        ):
            for part in range(8 // own):
                owner = base // own + part
                sums[stage][g, owner % 2, owner // 2, v] = value[part * own : (part + 1) * own]

    def get_rows(g, start):
        return jnp.concatenate(
            [
                from_code(
                    fluxes[g, (start // own + part) % 2, (start // own + part) // 2], steps
                )
                for part in range(8 // own)
            ],
            axis=0,
        ).reshape(8, 8, LANES)

    def pass_on(stage, g):
        near_copy(stage, g).wait_recv()
        mine[stage][g] = sums[stage][g, core, chip] + near[stage][g, chip]
        for j in range(1, chips):
            there = peer(j)
            both = sums[stage][g, core, there] + near[stage][g, there]
            pair[stage][g, there] = to_code(both.reshape(2, own * 8, LANES), steps)
            far_copy(stage, g, j).start()

    def total(stage, g):
        value = mine[stage][g]
        for j in range(1, chips):
            far_copy(stage, g, j).wait_recv()
            value = value + from_code(far[stage][g, j - 1], steps).reshape(value.shape)
        return value

    @pl.loop(0, groups)
    def _(g):
        for v in (0, 1):
            for start in range(0, half, 8):
                put(
                    0, g, v, start,
                    stacks[2 * g + v, 0, pl.ds(start, 8)], stacks[2 * g + v, 1, pl.ds(start, 8)],
                )
        near_copy(0, g).start()

        @pl.when(g > 0)
        def _():
            pass_on(0, g - 1)

    pass_on(0, groups - 1)

    def spread_flux(g):
        whole = total(0, g)
        flux = whole / (roll4(whole) + 1.0)
        flux = jnp.where(low, flux[0], roll4(flux[1])).reshape(own * 8, LANES)
        fluxes[g, core, chip] = to_code(flux, steps)
        for j in range(1, chips):
            flux_copy(g, j).start()

    def share_flux(g):
        for j in range(1, chips):
            flux_copy(g, j).wait_recv()
        flux_sibling(g).start()

    def reweight(g):
        flux_sibling(g).wait_recv()
        for start in range(0, half, 8):
            upper, lower = get_rows(g, start), get_rows(g, start + half)
            for v in (0, 1):
                if v == 0:
                    flux = jnp.where(low, upper, roll4(lower))
                else:
                    flux = jnp.where(low, roll4(upper), lower)
                signal_sum = jnp.zeros((8, 8, LANES), jnp.float32)
                depth_sum = jnp.zeros((8, 8, LANES), jnp.float32)
                for e in range(exposures):
                    signal = window(e, 2 * g + v, 0, start)
                    depth = window(e, 2 * g + v, 1, start)
                    residual = signal - flux * depth
                    more = depth + 1.0
                    weight = more / (more + residual * residual)
                    signal_sum += weight * signal
                    depth_sum += weight * depth
                put(1, g, v, start, signal_sum, depth_sum)
        near_copy(1, g).start()

    @pl.loop(0, groups + 3)
    def _(i):
        @pl.when(i < groups)
        def _():
            spread_flux(i)

        @pl.when((i >= 1) & (i < groups + 1))
        def _():
            share_flux(i - 1)

        @pl.when(i >= 3)
        def _():
            pass_on(1, i - 3)

        @pl.when((i >= 2) & (i < groups + 2))
        def _():
            reweight(i - 2)

    @pl.loop(0, groups)
    def _(g):
        whole = total(1, g)
        result = whole / jnp.sqrt(roll4(whole) + 1.0)
        final[...] = result.reshape(2 * own * 8, LANES)
        for v in (0, 1):
            for block in range(blocks):
                out[2 * g + v, :, block * LANES : (block + 1) * LANES] = final[
                    pl.ds(v * own * 8 + block, own, stride=8), :
                ]

    @pl.loop(0, groups)
    def _(g):
        for stage in (0, 1):
            near_copy(stage, g).wait_send()
            for j in range(1, chips):
                far_copy(stage, g, j).wait_send()
        for j in range(1, chips):
            flux_copy(g, j).wait_send()
        flux_sibling(g).wait_send()

    @pl.when(has_below)
    def _():
        for t in range(tiles):
            for array in (0, 1):
                edge_copy(t, array, 1).wait_send()

    @pl.when(has_above)
    def _():
        for t in range(tiles):
            for array in (0, 1):
                edge_copy(t, array, 0).wait_send()

        @pl.loop(0, exposures)
        def _(e):
            for array in (0, 1):
                full_copy(e, array).wait_send()


def per_device(count, strips, science, inv_var, psf_rows, psf_cols, row_shift, col_shift, ok):
    exposures, rows, columns = science.shape
    vels, taps = row_shift.shape[1], psf_rows.shape[1]
    chips, own, groups = count // 2, rows // count, vels // 2
    f32, bf16 = jnp.float32, jnp.bfloat16
    dma = lambda *shape: [pltpu.SemaphoreType.DMA(shape)] * 2
    radius = taps // 2
    tiles = exposures * radius // 16
    stage = [
        pltpu.VMEM((groups, 2, chips, 2, own, 8, LANES), f32),
        pltpu.VMEM((groups, chips, 2, own, 8, LANES), f32),
        pltpu.VMEM((groups, 2, own, 8, LANES), f32),
        pltpu.VMEM((groups, chips, 2, own * 8, LANES), jnp.int16),
        pltpu.VMEM((groups, chips - 1, 2, own * 8, LANES), jnp.int16),
    ]
    result = pl.pallas_call(
        functools.partial(kernel, (count, strips, exposures, rows, columns, vels, taps)),
        out_shape=jax.ShapeDtypeStruct((vels, own, columns), f32),
        in_specs=[pl.BlockSpec(memory_space=pl.ANY)] * 7,
        out_specs=pl.BlockSpec(memory_space=pltpu.VMEM),
        scratch_shapes=[
            pltpu.SMEM(psf_rows.shape, f32),
            pltpu.SMEM(psf_cols.shape, f32),
            pltpu.SMEM(row_shift.shape, jnp.int32),
            pltpu.SMEM(col_shift.shape, jnp.int32),
            pltpu.SMEM(ok.shape, jnp.int32),
            pltpu.VMEM(science.shape, bf16),
            pltpu.VMEM(science.shape, bf16),
            pltpu.SemaphoreType.DMA((7,)),
            pltpu.VMEM((2, exposures, SHIFT, columns), bf16),
            pltpu.VMEM((2, tiles, 16, columns), bf16),
            pltpu.VMEM((2, tiles, 16, columns), bf16),
            pltpu.VMEM((2, 2, tiles, 16, columns), bf16),
            pltpu.VMEM((2, 2, 16 // radius, 8, columns), f32),
            pltpu.VMEM((2, 16 + rows + SHIFT, columns), f32),
            pltpu.VMEM((4, exposures * rows, 8, LANES), f32),
            pltpu.VMEM((vels, 2, rows // 2, 8, LANES), f32),
            pltpu.VMEM((groups, 2, chips, own * 8, LANES), jnp.int16),
            pltpu.VMEM((2 * own * 8, LANES), f32),
            *stage,
            *stage,
            *dma(2, exposures),
            *dma(2, 2, tiles),
            *dma(2, groups),
            *dma(2, groups, chips - 1),
            *dma(groups, chips - 1),
            *dma(groups),
        ],
        compiler_params=pltpu.CompilerParams(
            collective_id=0, has_side_effects=True, vmem_limit_bytes=60 * 1024 * 1024
        ),
    )(psf_rows, psf_cols, row_shift, col_shift, ok, science, inv_var)
    return result.reshape(1, vels, own, columns)


def solution(mesh):
    from jax.sharding import PartitionSpec as P

    in_specs = (
        P(("field", "expo"), "strip", None),
        P(("field", "expo"), "strip", None),
        P(("field", "expo"), None),
        P(("field", "expo"), None),
        P(("field", "expo"), None),
        P(("field", "expo"), None),
        P(("field", "expo")),
    )
    return jax.shard_map(
        functools.partial(per_device, mesh.shape["expo"], mesh.shape["strip"]),
        mesh=mesh,
        in_specs=in_specs,
        out_specs=P("strip", "field", "expo", None),
        check_vma=False,
    )
```

```python
import functools
import math

import jax
import jax.numpy as jnp
from jax import lax
from jax.experimental import pallas as pl
from jax.experimental.pallas import tpu as pltpu

SHIFT = 16
LANES = 128
MESH = pl.DeviceIdType.MESH


LEAST = 2.0 ** -20
STEPS = 32700.0


def to_code(x, steps):
    level = jnp.log(1.0 + jnp.abs(x) * (1.0 / LEAST)) * steps + 0.5
    return jnp.where(x < 0, -level, level).astype(jnp.int32).astype(jnp.int16)


def from_code(code, steps):
    level = code.astype(jnp.int32).astype(jnp.float32)
    size = (jnp.exp(jnp.abs(level) * (1.0 / steps)) - 1.0) * LEAST
    return jnp.where(level < 0, -size, size)


def roll4(x):
    return pltpu.roll(x, 4, axis=x.ndim - 2)


def kernel(
    cfg,
    *refs,
):
    out, inputs, copied = refs[7], refs[:7], refs[8:15]
    row_taps, col_taps, row_shift, col_shift, usable, sci, inv = copied
    (in_s, below, tails, above, edge_out, edges, rows_in, maps, stacks, fluxes, final, *rest) = refs[15:]
    count, strips, exposures, rows, columns, vels, taps = cfg
    radius = taps // 2
    chips = count // 2
    own = rows // count
    half = rows // 2
    blocks = columns // LANES
    groups = vels // 2
    wide = columns + LANES
    map_rows = rows + SHIFT
    sums, near, mine, pair, far = zip(rest[0:5], rest[5:10])
    (full_s, full_r, edge_s, edge_r, near_s, near_r,
     far_s, far_r, flux_s, flux_r, fsib_s, fsib_r) = rest[10:]
    per_tile = 16 // radius
    most = 2.0 * exposures * 24.0 * taps * taps * 1.01
    steps = STEPS / math.log(1.0 + most / LEAST)
    tiles = exposures // per_tile

    me = lax.axis_index("expo")
    strip = lax.axis_index("strip")
    chip, core = me // 2, me % 2
    sibling = chip * 2 + (1 - core)
    has_above = strip > 0
    has_below = strip < strips - 1

    def peer(j):
        return (chip + j) % chips

    def full_copy(e, array):
        return pltpu.make_async_remote_copy(
            src_ref=(sci, inv)[array].at[e, pl.ds(0, SHIFT)], dst_ref=below.at[array, e],
            send_sem=full_s.at[array, e], recv_sem=full_r.at[array, e],
            device_id={"strip": strip - 1}, device_id_type=MESH,
        )

    def edge_copy(t, array, down):
        return pltpu.make_async_remote_copy(
            src_ref=edge_out.at[down, array, t], dst_ref=(tails, above)[down].at[array, t],
            send_sem=edge_s.at[down, array, t], recv_sem=edge_r.at[down, array, t],
            device_id={"strip": strip + 1 if down else strip - 1}, device_id_type=MESH,
        )

    def near_copy(stage, g):
        return pltpu.make_async_remote_copy(
            src_ref=sums[stage].at[g, 1 - core], dst_ref=near[stage].at[g],
            send_sem=near_s.at[stage, g], recv_sem=near_r.at[stage, g],
            device_id={"expo": sibling}, device_id_type=MESH,
        )

    def far_copy(stage, g, j):
        return pltpu.make_async_remote_copy(
            src_ref=pair[stage].at[g, peer(j)], dst_ref=far[stage].at[g, j - 1],
            send_sem=far_s.at[stage, g, j - 1], recv_sem=far_r.at[stage, g, j - 1],
            device_id={"expo": peer(j) * 2 + core}, device_id_type=MESH,
        )

    def flux_copy(g, j):
        mine = fluxes.at[g, core, chip]
        return pltpu.make_async_remote_copy(
            src_ref=mine, dst_ref=mine,
            send_sem=flux_s.at[g, j - 1], recv_sem=flux_r.at[g, j - 1],
            device_id={"expo": peer(j) * 2 + core}, device_id_type=MESH,
        )

    def flux_sibling(g):
        mine = fluxes.at[g, core]
        return pltpu.make_async_remote_copy(
            src_ref=mine, dst_ref=mine, send_sem=fsib_s.at[g], recv_sem=fsib_r.at[g],
            device_id={"expo": sibling}, device_id_type=MESH,
        )

    local = [
        pltpu.make_async_copy(inputs[k], copied[k], in_s.at[k]) for k in (5, 6, 0, 1, 2, 3, 4)
    ]
    for copy in local:
        copy.start()
    barrier = pltpu.get_barrier_semaphore()
    pl.semaphore_signal(barrier, inc=1, device_id={"expo": sibling}, device_id_type=MESH)
    for j in range(1, chips):
        pl.semaphore_signal(
            barrier, inc=1, device_id={"expo": peer(j) * 2 + core}, device_id_type=MESH
        )

    @pl.when(has_above)
    def _():
        pl.semaphore_signal(barrier, inc=1, device_id={"strip": strip - 1}, device_id_type=MESH)

    @pl.when(has_below)
    def _():
        pl.semaphore_signal(barrier, inc=1, device_id={"strip": strip + 1}, device_id_type=MESH)

    for copy in local[:2]:
        copy.wait()
    for array, source in enumerate((sci, inv)):
        for t in range(tiles):
            span = range(t * per_tile, (t + 1) * per_tile)
            for down, at in ((0, SHIFT), (1, rows - radius)):
                base = at // 16 * 16
                pieces = [
                    source[e, base : base + 16, :].astype(jnp.float32)[
                        at - base : at - base + radius
                    ]
                    for e in span
                ]
                edge_out[down, array, t] = jnp.concatenate(pieces, axis=0).astype(jnp.bfloat16)
    pl.semaphore_wait(barrier, chips + has_above.astype(jnp.int32) + has_below.astype(jnp.int32))

    @pl.when(has_below)
    def _():
        for t in range(tiles):
            for array in (0, 1):
                edge_copy(t, array, 1).start()

    @pl.when(has_above)
    def _():
        @pl.loop(0, tiles)
        def _(t):
            for array in (0, 1):
                edge_copy(t, array, 0).start()

            @pl.loop(0, per_tile)
            def _(q):
                for array in (0, 1):
                    full_copy(t * per_tile + q, array).start()

    @pl.when(jnp.logical_not(has_above))
    def _():
        above[...] = jnp.zeros_like(above)

    @pl.when(jnp.logical_not(has_below))
    def _():
        below[...] = jnp.zeros_like(below)
        tails[...] = jnp.zeros_like(tails)

    stacks[...] = jnp.zeros_like(stacks)
    for copy in local[2:]:
        copy.wait()

    lane = lax.broadcasted_iota(jnp.int32, (map_rows, wide), 1)
    row = lax.broadcasted_iota(jnp.int32, (map_rows, wide), 0)
    keep = (lane >= SHIFT) & (lane < SHIFT + columns) & ((row < rows) | has_below)

    low = lax.broadcasted_iota(jnp.int32, (1, 8, LANES), 1) < 4
    lane8 = lax.broadcasted_iota(jnp.int32, (1, 8, LANES), 2)

    def window(e, velocity, which, start):
        at = e * rows + row_shift[e, velocity] + start
        shift = col_shift[e, velocity] + SHIFT
        here = maps[2 * which, pl.ds(at, 8)]
        after = maps[2 * which + 1, pl.ds(at, 8)]
        mixed = jnp.where(jnp.broadcast_to(lane8 >= shift, here.shape), here, after)
        return pltpu.roll(mixed, (LANES - shift) & (LANES - 1), axis=2)

    flat = maps.reshape(4, exposures * rows * 8, LANES)

    @pl.loop(0, exposures)
    def _(e):
        tile_now, place_in_tile = e // per_tile, e % per_tile

        @pl.when(place_in_tile == 0)
        def _():
            @pl.when(has_below)
            def _():
                for array in (0, 1):
                    edge_copy(tile_now, array, 0).wait_recv()

            @pl.when(has_above)
            def _():
                for array in (0, 1):
                    edge_copy(tile_now, array, 1).wait_recv()

            for down, source in enumerate((tails, above)):
                for array in (0, 1):
                    tile = source[array, tile_now].astype(jnp.float32)
                    for q in range(per_tile):
                        piece = tile[q * radius : (q + 1) * radius]
                        edges[down, array, q] = jnp.concatenate([piece] * (8 // radius), axis=0)

        @pl.when(has_below)
        def _():
            for array in (0, 1):
                full_copy(e, array).wait_recv()

        for place, size, pick in (
            (0, 8, lambda k: edges[1, k, place_in_tile]),
            (8, rows, lambda k: (sci, inv)[k][e]),
            (8 + rows, SHIFT, lambda k: below[k, e]),
            (8 + rows + SHIFT, 8, lambda k: edges[0, k, place_in_tile]),
        ):
            inverse = pick(1).astype(jnp.float32)
            rows_in[0, pl.ds(place, size), :] = pick(0).astype(jnp.float32) * inverse
            rows_in[1, pl.ds(place, size), :] = inverse
        ok = usable[e].astype(jnp.float32)
        for which in (0, 1):
            def tap(ref, a):
                value = ref[e, a]
                return value * value if which else value

            filtered = tap(row_taps, 0) * rows_in[which, pl.ds(8 - radius, map_rows), :]
            for a in range(1, taps):
                filtered += tap(row_taps, a) * rows_in[which, pl.ds(8 - radius + a, map_rows), :]
            filtered = jnp.concatenate(
                [filtered, jnp.zeros((map_rows, LANES), jnp.float32)], axis=1
            )
            result = tap(col_taps, 0) * pltpu.roll(filtered, SHIFT + radius, axis=1)
            for b in range(1, taps):
                result += tap(col_taps, b) * pltpu.roll(filtered, SHIFT + radius - b, axis=1)
            result = jnp.where(keep, result, 0.0).astype(jnp.bfloat16).astype(jnp.float32) * ok
            for block in range(blocks + 1):
                for r in range(0, map_rows, 8):
                    tile = result[r : r + 8, block * LANES : (block + 1) * LANES]
                    for later in (0, 1):
                        sub = block - later
                        if sub < 0 or sub >= blocks:
                            continue
                        for at, shift in ((r, sub), (r - half, sub + 4)):
                            if 0 <= at < rows:
                                flat[2 * which + later,
                                     pl.ds((e * rows + at) * 8 + shift, 8, stride=8), :] = tile

        for velocity in range(vels):
            for which in (0, 1):
                for start in range(0, half, 8):
                    stacks[velocity, which, pl.ds(start, 8)] += window(e, velocity, which, start)

    def put(stage, g, v, start, signal, depth):
        for base, value in (
            (start, jnp.where(low, signal, roll4(depth))),
            (start + half, jnp.where(low, roll4(signal), depth)),
        ):
            for part in range(8 // own):
                owner = base // own + part
                sums[stage][g, owner % 2, owner // 2, v] = value[part * own : (part + 1) * own]

    def get_rows(g, start):
        return jnp.concatenate(
            [
                from_code(
                    fluxes[g, (start // own + part) % 2, (start // own + part) // 2], steps
                )
                for part in range(8 // own)
            ],
            axis=0,
        ).reshape(8, 8, LANES)

    def pass_on(stage, g):
        near_copy(stage, g).wait_recv()
        mine[stage][g] = sums[stage][g, core, chip] + near[stage][g, chip]
        for j in range(1, chips):
            there = peer(j)
            both = sums[stage][g, core, there] + near[stage][g, there]
            pair[stage][g, there] = to_code(both.reshape(2, own * 8, LANES), steps)
            far_copy(stage, g, j).start()

    def total(stage, g):
        value = mine[stage][g]
        for j in range(1, chips):
            far_copy(stage, g, j).wait_recv()
            value = value + from_code(far[stage][g, j - 1], steps).reshape(value.shape)
        return value

    @pl.loop(0, groups)
    def _(g):
        for v in (0, 1):
            for start in range(0, half, 8):
                put(
                    0, g, v, start,
                    stacks[2 * g + v, 0, pl.ds(start, 8)], stacks[2 * g + v, 1, pl.ds(start, 8)],
                )
        near_copy(0, g).start()

        @pl.when(g > 0)
        def _():
            pass_on(0, g - 1)

    pass_on(0, groups - 1)

    def spread_flux(g):
        whole = total(0, g)
        flux = whole / (roll4(whole) + 1.0)
        flux = jnp.where(low, flux[0], roll4(flux[1])).reshape(own * 8, LANES)
        fluxes[g, core, chip] = to_code(flux, steps)
        for j in range(1, chips):
            flux_copy(g, j).start()

    def share_flux(g):
        for j in range(1, chips):
            flux_copy(g, j).wait_recv()
        flux_sibling(g).start()

    def reweight(g):
        flux_sibling(g).wait_recv()
        for start in range(0, half, 8):
            upper, lower = get_rows(g, start), get_rows(g, start + half)
            for v in (0, 1):
                if v == 0:
                    flux = jnp.where(low, upper, roll4(lower))
                else:
                    flux = jnp.where(low, roll4(upper), lower)
                signal_sum = jnp.zeros((8, 8, LANES), jnp.float32)
                depth_sum = jnp.zeros((8, 8, LANES), jnp.float32)
                for e in range(exposures):
                    signal = window(e, 2 * g + v, 0, start)
                    depth = window(e, 2 * g + v, 1, start)
                    residual = signal - flux * depth
                    more = depth + 1.0
                    bottom = more + residual * residual
                    guess = pl.reciprocal(bottom, approx=True)
                    weight = more * (guess * (2.0 - bottom * guess))
                    signal_sum += weight * signal
                    depth_sum += weight * depth
                put(1, g, v, start, signal_sum, depth_sum)
        near_copy(1, g).start()

    @pl.loop(0, groups + 3)
    def _(i):
        @pl.when(i < groups)
        def _():
            spread_flux(i)

        @pl.when((i >= 1) & (i < groups + 1))
        def _():
            share_flux(i - 1)

        @pl.when(i >= 3)
        def _():
            pass_on(1, i - 3)

        @pl.when((i >= 2) & (i < groups + 2))
        def _():
            reweight(i - 2)

    @pl.loop(0, groups)
    def _(g):
        whole = total(1, g)
        result = whole / jnp.sqrt(roll4(whole) + 1.0)
        final[...] = result.reshape(2 * own * 8, LANES)
        for v in (0, 1):
            for block in range(blocks):
                out[2 * g + v, :, block * LANES : (block + 1) * LANES] = final[
                    pl.ds(v * own * 8 + block, own, stride=8), :
                ]

    @pl.loop(0, groups)
    def _(g):
        for stage in (0, 1):
            near_copy(stage, g).wait_send()
            for j in range(1, chips):
                far_copy(stage, g, j).wait_send()
        for j in range(1, chips):
            flux_copy(g, j).wait_send()
        flux_sibling(g).wait_send()

    @pl.when(has_below)
    def _():
        for t in range(tiles):
            for array in (0, 1):
                edge_copy(t, array, 1).wait_send()

    @pl.when(has_above)
    def _():
        for t in range(tiles):
            for array in (0, 1):
                edge_copy(t, array, 0).wait_send()

        @pl.loop(0, exposures)
        def _(e):
            for array in (0, 1):
                full_copy(e, array).wait_send()


def per_device(count, strips, science, inv_var, psf_rows, psf_cols, row_shift, col_shift, ok):
    exposures, rows, columns = science.shape
    vels, taps = row_shift.shape[1], psf_rows.shape[1]
    chips, own, groups = count // 2, rows // count, vels // 2
    f32, bf16 = jnp.float32, jnp.bfloat16
    dma = lambda *shape: [pltpu.SemaphoreType.DMA(shape)] * 2
    radius = taps // 2
    tiles = exposures * radius // 16
    stage = [
        pltpu.VMEM((groups, 2, chips, 2, own, 8, LANES), f32),
        pltpu.VMEM((groups, chips, 2, own, 8, LANES), f32),
        pltpu.VMEM((groups, 2, own, 8, LANES), f32),
        pltpu.VMEM((groups, chips, 2, own * 8, LANES), jnp.int16),
        pltpu.VMEM((groups, chips - 1, 2, own * 8, LANES), jnp.int16),
    ]
    result = pl.pallas_call(
        functools.partial(kernel, (count, strips, exposures, rows, columns, vels, taps)),
        out_shape=jax.ShapeDtypeStruct((vels, own, columns), f32),
        in_specs=[pl.BlockSpec(memory_space=pl.ANY)] * 7,
        out_specs=pl.BlockSpec(memory_space=pltpu.VMEM),
        scratch_shapes=[
            pltpu.SMEM(psf_rows.shape, f32),
            pltpu.SMEM(psf_cols.shape, f32),
            pltpu.SMEM(row_shift.shape, jnp.int32),
            pltpu.SMEM(col_shift.shape, jnp.int32),
            pltpu.SMEM(ok.shape, jnp.int32),
            pltpu.VMEM(science.shape, bf16),
            pltpu.VMEM(science.shape, bf16),
            pltpu.SemaphoreType.DMA((7,)),
            pltpu.VMEM((2, exposures, SHIFT, columns), bf16),
            pltpu.VMEM((2, tiles, 16, columns), bf16),
            pltpu.VMEM((2, tiles, 16, columns), bf16),
            pltpu.VMEM((2, 2, tiles, 16, columns), bf16),
            pltpu.VMEM((2, 2, 16 // radius, 8, columns), f32),
            pltpu.VMEM((2, 16 + rows + SHIFT, columns), f32),
            pltpu.VMEM((4, exposures * rows, 8, LANES), f32),
            pltpu.VMEM((vels, 2, rows // 2, 8, LANES), f32),
            pltpu.VMEM((groups, 2, chips, own * 8, LANES), jnp.int16),
            pltpu.VMEM((2 * own * 8, LANES), f32),
            *stage,
            *stage,
            *dma(2, exposures),
            *dma(2, 2, tiles),
            *dma(2, groups),
            *dma(2, groups, chips - 1),
            *dma(groups, chips - 1),
            *dma(groups),
        ],
        compiler_params=pltpu.CompilerParams(
            collective_id=0, has_side_effects=True, vmem_limit_bytes=60 * 1024 * 1024
        ),
    )(psf_rows, psf_cols, row_shift, col_shift, ok, science, inv_var)
    return result.reshape(1, vels, own, columns)


def solution(mesh):
    from jax.sharding import PartitionSpec as P

    in_specs = (
        P(("field", "expo"), "strip", None),
        P(("field", "expo"), "strip", None),
        P(("field", "expo"), None),
        P(("field", "expo"), None),
        P(("field", "expo"), None),
        P(("field", "expo"), None),
        P(("field", "expo")),
    )
    return jax.shard_map(
        functools.partial(per_device, mesh.shape["expo"], mesh.shape["strip"]),
        mesh=mesh,
        in_specs=in_specs,
        out_specs=P("strip", "field", "expo", None),
        check_vma=False,
    )
```

```python
import functools
import math

import jax
import jax.numpy as jnp
from jax import lax
from jax.experimental import pallas as pl
from jax.experimental.pallas import tpu as pltpu

SHIFT = 16
LANES = 128
MESH = pl.DeviceIdType.MESH


LEAST = 2.0 ** -20
STEPS = 32700.0


def to_code(x, steps):
    level = jnp.log(1.0 + jnp.abs(x) * (1.0 / LEAST)) * steps + 0.5
    return jnp.where(x < 0, -level, level).astype(jnp.int32).astype(jnp.int16)


def from_code(code, steps):
    level = code.astype(jnp.int32).astype(jnp.float32)
    size = (jnp.exp(jnp.abs(level) * (1.0 / steps)) - 1.0) * LEAST
    return jnp.where(level < 0, -size, size)


def roll4(x):
    return pltpu.roll(x, 4, axis=x.ndim - 2)


def kernel(
    cfg,
    *refs,
):
    out, inputs, copied = refs[7], refs[:7], refs[8:15]
    row_taps, col_taps, row_shift, col_shift, usable, sci, inv = copied
    (in_s, below, tails, above, edge_out, edges, raw, maps, stacks, fluxes, final, *rest) = refs[15:]
    count, strips, exposures, rows, columns, vels, taps = cfg
    radius = taps // 2
    chips = count // 2
    own = rows // count
    half = rows // 2
    blocks = columns // LANES
    groups = vels // 2
    apart = (rows + SHIFT) // 2
    sums, near, mine, pair, far = zip(rest[0:5], rest[5:10])
    (full_s, full_r, edge_s, edge_r, near_s, near_r,
     far_s, far_r, flux_s, flux_r, fsib_s, fsib_r) = rest[10:]
    per_tile = 16 // radius
    most = 2.0 * exposures * 24.0 * taps * taps * 1.01
    steps = STEPS / math.log(1.0 + most / LEAST)
    tiles = exposures // per_tile

    me = lax.axis_index("expo")
    strip = lax.axis_index("strip")
    chip, core = me // 2, me % 2
    sibling = chip * 2 + (1 - core)
    has_above = strip > 0
    has_below = strip < strips - 1

    def peer(j):
        return (chip + j) % chips

    def full_copy(e, array):
        return pltpu.make_async_remote_copy(
            src_ref=(sci, inv)[array].at[e, pl.ds(0, SHIFT)], dst_ref=below.at[array, e],
            send_sem=full_s.at[array, e], recv_sem=full_r.at[array, e],
            device_id={"strip": strip - 1}, device_id_type=MESH,
        )

    def edge_copy(t, array, down):
        return pltpu.make_async_remote_copy(
            src_ref=edge_out.at[down, array, t], dst_ref=(tails, above)[down].at[array, t],
            send_sem=edge_s.at[down, array, t], recv_sem=edge_r.at[down, array, t],
            device_id={"strip": strip + 1 if down else strip - 1}, device_id_type=MESH,
        )

    def near_copy(stage, g):
        return pltpu.make_async_remote_copy(
            src_ref=sums[stage].at[g, 1 - core], dst_ref=near[stage].at[g],
            send_sem=near_s.at[stage, g], recv_sem=near_r.at[stage, g],
            device_id={"expo": sibling}, device_id_type=MESH,
        )

    def far_copy(stage, g, j):
        return pltpu.make_async_remote_copy(
            src_ref=pair[stage].at[g, peer(j)], dst_ref=far[stage].at[g, j - 1],
            send_sem=far_s.at[stage, g, j - 1], recv_sem=far_r.at[stage, g, j - 1],
            device_id={"expo": peer(j) * 2 + core}, device_id_type=MESH,
        )

    def flux_copy(g, j):
        mine = fluxes.at[g, core, chip]
        return pltpu.make_async_remote_copy(
            src_ref=mine, dst_ref=mine,
            send_sem=flux_s.at[g, j - 1], recv_sem=flux_r.at[g, j - 1],
            device_id={"expo": peer(j) * 2 + core}, device_id_type=MESH,
        )

    def flux_sibling(g):
        mine = fluxes.at[g, core]
        return pltpu.make_async_remote_copy(
            src_ref=mine, dst_ref=mine, send_sem=fsib_s.at[g], recv_sem=fsib_r.at[g],
            device_id={"expo": sibling}, device_id_type=MESH,
        )

    local = [
        pltpu.make_async_copy(inputs[k], copied[k], in_s.at[k]) for k in (5, 6, 0, 1, 2, 3, 4)
    ]
    for copy in local:
        copy.start()
    barrier = pltpu.get_barrier_semaphore()
    pl.semaphore_signal(barrier, inc=1, device_id={"expo": sibling}, device_id_type=MESH)
    for j in range(1, chips):
        pl.semaphore_signal(
            barrier, inc=1, device_id={"expo": peer(j) * 2 + core}, device_id_type=MESH
        )

    @pl.when(has_above)
    def _():
        pl.semaphore_signal(barrier, inc=1, device_id={"strip": strip - 1}, device_id_type=MESH)

    @pl.when(has_below)
    def _():
        pl.semaphore_signal(barrier, inc=1, device_id={"strip": strip + 1}, device_id_type=MESH)

    for copy in local[:2]:
        copy.wait()
    for array, source in enumerate((sci, inv)):
        for t in range(tiles):
            span = range(t * per_tile, (t + 1) * per_tile)
            for down, at in ((0, SHIFT), (1, rows - radius)):
                base = at // 16 * 16
                pieces = [
                    source[e, base : base + 16, :].astype(jnp.float32)[
                        at - base : at - base + radius
                    ]
                    for e in span
                ]
                edge_out[down, array, t] = jnp.concatenate(pieces, axis=0).astype(jnp.bfloat16)
    pl.semaphore_wait(barrier, chips + has_above.astype(jnp.int32) + has_below.astype(jnp.int32))

    @pl.when(has_below)
    def _():
        for t in range(tiles):
            for array in (0, 1):
                edge_copy(t, array, 1).start()

    @pl.when(has_above)
    def _():
        @pl.loop(0, tiles)
        def _(t):
            for array in (0, 1):
                edge_copy(t, array, 0).start()

            @pl.loop(0, per_tile)
            def _(q):
                for array in (0, 1):
                    full_copy(t * per_tile + q, array).start()

    @pl.when(jnp.logical_not(has_above))
    def _():
        above[...] = jnp.zeros_like(above)

    @pl.when(jnp.logical_not(has_below))
    def _():
        below[...] = jnp.zeros_like(below)
        tails[...] = jnp.zeros_like(tails)

    stacks[...] = jnp.zeros_like(stacks)
    for copy in local[2:]:
        copy.wait()

    sub = lax.broadcasted_iota(jnp.int32, (1, 8, LANES), 1)
    lane = lax.broadcasted_iota(jnp.int32, (1, 8, LANES), 2)
    low = sub < 4
    first_block, last_block = sub % 4 == 0, sub % 4 == 3
    span = exposures * rows

    def choose(mask, x, y):
        return jnp.where(jnp.broadcast_to(mask, x.shape), x, y)

    def next_blocks(x):
        return choose(last_block, jnp.zeros_like(x), pltpu.roll(x, 7, axis=1))

    def previous_blocks(x):
        return choose(first_block, jnp.zeros_like(x), pltpu.roll(x, 1, axis=1))

    def window(e, velocity, which, start):
        shift = col_shift[e, velocity]
        left = jnp.where(shift < 0, 0, span) + e * rows + row_shift[e, velocity] + start
        here = maps[which, pl.ds(left, 8)]
        after = maps[which, pl.ds(left + span, 8)]
        mixed = choose(lane >= (shift & (LANES - 1)), here, after)
        return pltpu.roll(mixed, (-shift) & (LANES - 1), axis=2)

    raw_rows = raw.reshape(2, raw.shape[1] * 8, LANES)

    @pl.loop(0, exposures)
    def _(e):
        tile_now, place_in_tile = e // per_tile, e % per_tile

        @pl.when(place_in_tile == 0)
        def _():
            @pl.when(has_below)
            def _():
                for array in (0, 1):
                    edge_copy(tile_now, array, 0).wait_recv()

            @pl.when(has_above)
            def _():
                for array in (0, 1):
                    edge_copy(tile_now, array, 1).wait_recv()

            for down, source in enumerate((tails, above)):
                for array in (0, 1):
                    tile = source[array, tile_now].astype(jnp.float32)
                    for q in range(per_tile):
                        piece = tile[q * radius : (q + 1) * radius]
                        edges[down, array, q] = jnp.concatenate([piece] * (8 // radius), axis=0)

        @pl.when(has_below)
        def _():
            for array in (0, 1):
                full_copy(e, array).wait_recv()

        for first, pick in (
            (-8, lambda k: edges[1, k, place_in_tile]),
            *((r, lambda k, r=r: (sci, inv)[k][e, r : r + 16, :]) for r in range(0, rows, 16)),
            (rows, lambda k: below[k, e]),
            (rows + SHIFT, lambda k: edges[0, k, place_in_tile]),
        ):
            inverse = pick(1).astype(jnp.float32)
            weighted = pick(0).astype(jnp.float32) * inverse
            for which, value in enumerate((weighted, inverse)):
                for r in range(first, first + value.shape[0], 8):
                    for at, shift in ((r + 8, 0), (r + 8 - apart, 4)):
                        if 0 <= at <= apart + 8:
                            for block in range(blocks):
                                raw_rows[
                                    which, pl.ds(at * 8 + shift + block, 8, stride=8), :
                                ] = value[
                                    r - first : r - first + 8,
                                    block * LANES : (block + 1) * LANES,
                                ]
        ok = usable[e].astype(jnp.float32)
        ok_last = jnp.where(low, ok, jnp.where(has_below, ok, 0.0))
        for which in (0, 1):
            def tap(ref, a):
                value = ref[e, a]
                return value * value if which else value

            filtered = tap(row_taps, 0) * raw[which, pl.ds(8 - radius, apart)]
            for a in range(1, taps):
                filtered += tap(row_taps, a) * raw[which, pl.ds(8 - radius + a, apart)]
            after, before = next_blocks(filtered), previous_blocks(filtered)
            result = tap(col_taps, radius) * filtered
            for d in range(1, radius + 1):
                right = pltpu.roll(choose(lane >= d, filtered, after), LANES - d, axis=2)
                left = pltpu.roll(choose(lane >= LANES - d, before, filtered), d, axis=2)
                result += tap(col_taps, radius + d) * right + tap(col_taps, radius - d) * left
            result = result.astype(jnp.bfloat16).astype(jnp.float32)
            inside = rows - apart
            result = jnp.concatenate([result[:inside] * ok, result[inside:] * ok_last], axis=0)
            step = apart - half
            table = jnp.concatenate(
                [
                    choose(low, result[:step], roll4(result[half:])),
                    choose(low, result[step:], result[:half]),
                    choose(low, roll4(result[:inside]), result[half : half + inside]),
                ],
                axis=0,
            )
            for copy, value in enumerate((previous_blocks(table), table, next_blocks(table))):
                maps[which, pl.ds(copy * span + e * rows, rows)] = value

        for velocity in range(vels):
            for which in (0, 1):
                for start in range(0, half, 8):
                    stacks[velocity, which, pl.ds(start, 8)] += window(e, velocity, which, start)

    def put(stage, g, v, start, signal, depth):
        for base, value in (
            (start, jnp.where(low, signal, roll4(depth))),
            (start + half, jnp.where(low, roll4(signal), depth)),
        ):
            for part in range(8 // own):
                owner = base // own + part
                sums[stage][g, owner % 2, owner // 2, v] = value[part * own : (part + 1) * own]

    def get_rows(g, start):
        return jnp.concatenate(
            [
                from_code(
                    fluxes[g, (start // own + part) % 2, (start // own + part) // 2], steps
                )
                for part in range(8 // own)
            ],
            axis=0,
        ).reshape(8, 8, LANES)

    def pass_on(stage, g):
        near_copy(stage, g).wait_recv()
        mine[stage][g] = sums[stage][g, core, chip] + near[stage][g, chip]
        for j in range(1, chips):
            there = peer(j)
            both = sums[stage][g, core, there] + near[stage][g, there]
            pair[stage][g, there] = to_code(both.reshape(2, own * 8, LANES), steps)
            far_copy(stage, g, j).start()

    def total(stage, g):
        value = mine[stage][g]
        for j in range(1, chips):
            far_copy(stage, g, j).wait_recv()
            value = value + from_code(far[stage][g, j - 1], steps).reshape(value.shape)
        return value

    @pl.loop(0, groups)
    def _(g):
        for v in (0, 1):
            for start in range(0, half, 8):
                put(
                    0, g, v, start,
                    stacks[2 * g + v, 0, pl.ds(start, 8)], stacks[2 * g + v, 1, pl.ds(start, 8)],
                )
        near_copy(0, g).start()

        @pl.when(g > 0)
        def _():
            pass_on(0, g - 1)

    pass_on(0, groups - 1)

    def spread_flux(g):
        whole = total(0, g)
        flux = whole / (roll4(whole) + 1.0)
        flux = jnp.where(low, flux[0], roll4(flux[1])).reshape(own * 8, LANES)
        fluxes[g, core, chip] = to_code(flux, steps)
        for j in range(1, chips):
            flux_copy(g, j).start()

    def share_flux(g):
        for j in range(1, chips):
            flux_copy(g, j).wait_recv()
        flux_sibling(g).start()

    def reweight(g):
        flux_sibling(g).wait_recv()
        for start in range(0, half, 8):
            upper, lower = get_rows(g, start), get_rows(g, start + half)
            for v in (0, 1):
                if v == 0:
                    flux = jnp.where(low, upper, roll4(lower))
                else:
                    flux = jnp.where(low, roll4(upper), lower)
                signal_sum = jnp.zeros((8, 8, LANES), jnp.float32)
                depth_sum = jnp.zeros((8, 8, LANES), jnp.float32)
                for e in range(exposures):
                    signal = window(e, 2 * g + v, 0, start)
                    depth = window(e, 2 * g + v, 1, start)
                    residual = signal - flux * depth
                    more = depth + 1.0
                    bottom = more + residual * residual
                    guess = pl.reciprocal(bottom, approx=True)
                    weight = more * (guess * (2.0 - bottom * guess))
                    signal_sum += weight * signal
                    depth_sum += weight * depth
                put(1, g, v, start, signal_sum, depth_sum)
        near_copy(1, g).start()

    @pl.loop(0, groups + 3)
    def _(i):
        @pl.when(i < groups)
        def _():
            spread_flux(i)

        @pl.when((i >= 1) & (i < groups + 1))
        def _():
            share_flux(i - 1)

        @pl.when(i >= 3)
        def _():
            pass_on(1, i - 3)

        @pl.when((i >= 2) & (i < groups + 2))
        def _():
            reweight(i - 2)

    @pl.loop(0, groups)
    def _(g):
        whole = total(1, g)
        result = whole / jnp.sqrt(roll4(whole) + 1.0)
        final[...] = result.reshape(2 * own * 8, LANES)
        for v in (0, 1):
            for block in range(blocks):
                out[2 * g + v, :, block * LANES : (block + 1) * LANES] = final[
                    pl.ds(v * own * 8 + block, own, stride=8), :
                ]

    @pl.loop(0, groups)
    def _(g):
        for stage in (0, 1):
            near_copy(stage, g).wait_send()
            for j in range(1, chips):
                far_copy(stage, g, j).wait_send()
        for j in range(1, chips):
            flux_copy(g, j).wait_send()
        flux_sibling(g).wait_send()

    @pl.when(has_below)
    def _():
        for t in range(tiles):
            for array in (0, 1):
                edge_copy(t, array, 1).wait_send()

    @pl.when(has_above)
    def _():
        for t in range(tiles):
            for array in (0, 1):
                edge_copy(t, array, 0).wait_send()

        @pl.loop(0, exposures)
        def _(e):
            for array in (0, 1):
                full_copy(e, array).wait_send()


def per_device(count, strips, science, inv_var, psf_rows, psf_cols, row_shift, col_shift, ok):
    exposures, rows, columns = science.shape
    vels, taps = row_shift.shape[1], psf_rows.shape[1]
    chips, own, groups = count // 2, rows // count, vels // 2
    f32, bf16 = jnp.float32, jnp.bfloat16
    dma = lambda *shape: [pltpu.SemaphoreType.DMA(shape)] * 2
    radius = taps // 2
    tiles = exposures * radius // 16
    stage = [
        pltpu.VMEM((groups, 2, chips, 2, own, 8, LANES), f32),
        pltpu.VMEM((groups, chips, 2, own, 8, LANES), f32),
        pltpu.VMEM((groups, 2, own, 8, LANES), f32),
        pltpu.VMEM((groups, chips, 2, own * 8, LANES), jnp.int16),
        pltpu.VMEM((groups, chips - 1, 2, own * 8, LANES), jnp.int16),
    ]
    result = pl.pallas_call(
        functools.partial(kernel, (count, strips, exposures, rows, columns, vels, taps)),
        out_shape=jax.ShapeDtypeStruct((vels, own, columns), f32),
        in_specs=[pl.BlockSpec(memory_space=pl.ANY)] * 7,
        out_specs=pl.BlockSpec(memory_space=pltpu.VMEM),
        scratch_shapes=[
            pltpu.SMEM(psf_rows.shape, f32),
            pltpu.SMEM(psf_cols.shape, f32),
            pltpu.SMEM(row_shift.shape, jnp.int32),
            pltpu.SMEM(col_shift.shape, jnp.int32),
            pltpu.SMEM(ok.shape, jnp.int32),
            pltpu.VMEM(science.shape, bf16),
            pltpu.VMEM(science.shape, bf16),
            pltpu.SemaphoreType.DMA((7,)),
            pltpu.VMEM((2, exposures, SHIFT, columns), bf16),
            pltpu.VMEM((2, tiles, 16, columns), bf16),
            pltpu.VMEM((2, tiles, 16, columns), bf16),
            pltpu.VMEM((2, 2, tiles, 16, columns), bf16),
            pltpu.VMEM((2, 2, 16 // radius, 8, columns), f32),
            pltpu.VMEM((2, (rows + SHIFT) // 2 + 16, 8, LANES), f32),
            pltpu.VMEM((2, 3 * exposures * rows, 8, LANES), f32),
            pltpu.VMEM((vels, 2, rows // 2, 8, LANES), f32),
            pltpu.VMEM((groups, 2, chips, own * 8, LANES), jnp.int16),
            pltpu.VMEM((2 * own * 8, LANES), f32),
            *stage,
            *stage,
            *dma(2, exposures),
            *dma(2, 2, tiles),
            *dma(2, groups),
            *dma(2, groups, chips - 1),
            *dma(groups, chips - 1),
            *dma(groups),
        ],
        compiler_params=pltpu.CompilerParams(
            collective_id=0, has_side_effects=True, vmem_limit_bytes=60 * 1024 * 1024
        ),
    )(psf_rows, psf_cols, row_shift, col_shift, ok, science, inv_var)
    return result.reshape(1, vels, own, columns)


def solution(mesh):
    from jax.sharding import PartitionSpec as P

    in_specs = (
        P(("field", "expo"), "strip", None),
        P(("field", "expo"), "strip", None),
        P(("field", "expo"), None),
        P(("field", "expo"), None),
        P(("field", "expo"), None),
        P(("field", "expo"), None),
        P(("field", "expo")),
    )
    return jax.shard_map(
        functools.partial(per_device, mesh.shape["expo"], mesh.shape["strip"]),
        mesh=mesh,
        in_specs=in_specs,
        out_specs=P("strip", "field", "expo", None),
        check_vma=False,
    )
```

```python
import functools
import math

import jax
import jax.numpy as jnp
from jax import lax
from jax.experimental import pallas as pl
from jax.experimental.pallas import tpu as pltpu

SHIFT = 16
LANES = 128
MESH = pl.DeviceIdType.MESH


LEAST = 2.0 ** -20
STEPS = 32700.0


def to_code(x, steps):
    level = jnp.log(1.0 + jnp.abs(x) * (1.0 / LEAST)) * steps + 0.5
    return jnp.where(x < 0, -level, level).astype(jnp.int32).astype(jnp.int16)


def from_code(code, steps):
    level = code.astype(jnp.int32).astype(jnp.float32)
    size = (jnp.exp(jnp.abs(level) * (1.0 / steps)) - 1.0) * LEAST
    return jnp.where(level < 0, -size, size)


def roll4(x):
    return pltpu.roll(x, 4, axis=x.ndim - 2)


def kernel(
    cfg,
    *refs,
):
    out, inputs, copied = refs[7], refs[:7], refs[8:15]
    row_taps, col_taps, row_shift, col_shift, usable, sci, inv = copied
    (in_s, below, tails, above, edge_out, edges, raw, maps, stacks, fluxes, final, *rest) = refs[15:]
    count, strips, exposures, rows, columns, vels, taps = cfg
    radius = taps // 2
    chips = count // 2
    own = rows // count
    half = rows // 2
    blocks = columns // LANES
    groups = vels // 2
    apart = (rows + SHIFT) // 2
    sums, near, mine, pair, far = zip(rest[0:5], rest[5:10])
    (full_s, full_r, edge_s, edge_r, near_s, near_r,
     far_s, far_r, flux_s, flux_r, fsib_s, fsib_r) = rest[10:]
    per_tile = 16 // radius
    most = 2.0 * exposures * 24.0 * taps * taps * 1.01
    steps = STEPS / math.log(1.0 + most / LEAST)
    tiles = exposures // per_tile

    me = lax.axis_index("expo")
    strip = lax.axis_index("strip")
    chip, core = me // 2, me % 2
    sibling = chip * 2 + (1 - core)
    has_above = strip > 0
    has_below = strip < strips - 1

    def peer(j):
        return (chip + j) % chips

    def full_copy(e, array):
        return pltpu.make_async_remote_copy(
            src_ref=(sci, inv)[array].at[e, pl.ds(0, SHIFT)], dst_ref=below.at[array, e],
            send_sem=full_s.at[array, e], recv_sem=full_r.at[array, e],
            device_id={"strip": strip - 1}, device_id_type=MESH,
        )

    def edge_copy(t, array, down):
        return pltpu.make_async_remote_copy(
            src_ref=edge_out.at[down, array, t], dst_ref=(tails, above)[down].at[array, t],
            send_sem=edge_s.at[down, array, t], recv_sem=edge_r.at[down, array, t],
            device_id={"strip": strip + 1 if down else strip - 1}, device_id_type=MESH,
        )

    def near_copy(stage, g):
        return pltpu.make_async_remote_copy(
            src_ref=sums[stage].at[g, 1 - core], dst_ref=near[stage].at[g],
            send_sem=near_s.at[stage, g], recv_sem=near_r.at[stage, g],
            device_id={"expo": sibling}, device_id_type=MESH,
        )

    def far_copy(stage, g, j):
        return pltpu.make_async_remote_copy(
            src_ref=pair[stage].at[g, peer(j)], dst_ref=far[stage].at[g, j - 1],
            send_sem=far_s.at[stage, g, j - 1], recv_sem=far_r.at[stage, g, j - 1],
            device_id={"expo": peer(j) * 2 + core}, device_id_type=MESH,
        )

    def flux_copy(g, j):
        mine = fluxes.at[g, core, chip]
        return pltpu.make_async_remote_copy(
            src_ref=mine, dst_ref=mine,
            send_sem=flux_s.at[g, j - 1], recv_sem=flux_r.at[g, j - 1],
            device_id={"expo": peer(j) * 2 + core}, device_id_type=MESH,
        )

    def flux_sibling(g):
        mine = fluxes.at[g, core]
        return pltpu.make_async_remote_copy(
            src_ref=mine, dst_ref=mine, send_sem=fsib_s.at[g], recv_sem=fsib_r.at[g],
            device_id={"expo": sibling}, device_id_type=MESH,
        )

    local = [
        pltpu.make_async_copy(inputs[k], copied[k], in_s.at[k]) for k in (5, 6, 0, 1, 2, 3, 4)
    ]
    for copy in local:
        copy.start()
    barrier = pltpu.get_barrier_semaphore()
    pl.semaphore_signal(barrier, inc=1, device_id={"expo": sibling}, device_id_type=MESH)
    for j in range(1, chips):
        pl.semaphore_signal(
            barrier, inc=1, device_id={"expo": peer(j) * 2 + core}, device_id_type=MESH
        )

    @pl.when(has_above)
    def _():
        pl.semaphore_signal(barrier, inc=1, device_id={"strip": strip - 1}, device_id_type=MESH)

    @pl.when(has_below)
    def _():
        pl.semaphore_signal(barrier, inc=1, device_id={"strip": strip + 1}, device_id_type=MESH)

    for copy in local[:2]:
        copy.wait()
    for array, source in enumerate((sci, inv)):
        for t in range(tiles):
            span = range(t * per_tile, (t + 1) * per_tile)
            for down, at in ((0, SHIFT), (1, rows - radius)):
                base = at // 16 * 16
                pieces = [
                    source[e, base : base + 16, :].astype(jnp.float32)[
                        at - base : at - base + radius
                    ]
                    for e in span
                ]
                edge_out[down, array, t] = jnp.concatenate(pieces, axis=0).astype(jnp.bfloat16)
    pl.semaphore_wait(barrier, chips + has_above.astype(jnp.int32) + has_below.astype(jnp.int32))

    @pl.when(has_below)
    def _():
        for t in range(tiles):
            for array in (0, 1):
                edge_copy(t, array, 1).start()

    @pl.when(has_above)
    def _():
        @pl.loop(0, tiles)
        def _(t):
            for array in (0, 1):
                edge_copy(t, array, 0).start()

            @pl.loop(0, per_tile)
            def _(q):
                for array in (0, 1):
                    full_copy(t * per_tile + q, array).start()

    @pl.when(jnp.logical_not(has_above))
    def _():
        above[...] = jnp.zeros_like(above)

    @pl.when(jnp.logical_not(has_below))
    def _():
        below[...] = jnp.zeros_like(below)
        tails[...] = jnp.zeros_like(tails)

    stacks[...] = jnp.zeros_like(stacks)
    for copy in local[2:]:
        copy.wait()

    sub = lax.broadcasted_iota(jnp.int32, (1, 8, LANES), 1)
    lane = lax.broadcasted_iota(jnp.int32, (1, 8, LANES), 2)
    low = sub < 4
    first_block, last_block = sub % 4 == 0, sub % 4 == 3
    span = exposures * rows

    def choose(mask, x, y):
        return jnp.where(jnp.broadcast_to(mask, x.shape), x, y)

    def next_blocks(x):
        return choose(last_block, jnp.zeros_like(x), pltpu.roll(x, 7, axis=1))

    def previous_blocks(x):
        return choose(first_block, jnp.zeros_like(x), pltpu.roll(x, 1, axis=1))

    def window(e, velocity, which, start):
        shift = col_shift[e, velocity]
        left = jnp.where(shift < 0, 0, span) + e * rows + row_shift[e, velocity] + start
        here = maps[which, pl.ds(left, 8)]
        after = maps[which, pl.ds(left + span, 8)]
        mixed = choose(lane >= (shift & (LANES - 1)), here, after)
        return pltpu.roll(mixed, (-shift) & (LANES - 1), axis=2)

    raw_rows = raw.reshape(2, raw.shape[1] * 8, LANES)

    @pl.loop(0, exposures)
    def _(e):
        tile_now, place_in_tile = e // per_tile, e % per_tile

        @pl.when(place_in_tile == 0)
        def _():
            @pl.when(has_below)
            def _():
                for array in (0, 1):
                    edge_copy(tile_now, array, 0).wait_recv()

            @pl.when(has_above)
            def _():
                for array in (0, 1):
                    edge_copy(tile_now, array, 1).wait_recv()

            for down, source in enumerate((tails, above)):
                for array in (0, 1):
                    tile = source[array, tile_now].astype(jnp.float32)
                    for q in range(per_tile):
                        piece = tile[q * radius : (q + 1) * radius]
                        edges[down, array, q] = jnp.concatenate([piece] * (8 // radius), axis=0)

        @pl.when(has_below)
        def _():
            for array in (0, 1):
                full_copy(e, array).wait_recv()

        for first, pick in (
            (-8, lambda k: edges[1, k, place_in_tile]),
            *((r, lambda k, r=r: (sci, inv)[k][e, r : r + 16, :]) for r in range(0, rows, 16)),
            (rows, lambda k: below[k, e]),
            (rows + SHIFT, lambda k: edges[0, k, place_in_tile]),
        ):
            inverse = pick(1).astype(jnp.float32)
            weighted = pick(0).astype(jnp.float32) * inverse
            for which, value in enumerate((weighted, inverse)):
                for r in range(first, first + value.shape[0], 8):
                    for at, shift in ((r + 8, 0), (r + 8 - apart, 4)):
                        if 0 <= at <= apart + 8:
                            for block in range(blocks):
                                raw_rows[
                                    which, pl.ds(at * 8 + shift + block, 8, stride=8), :
                                ] = value[
                                    r - first : r - first + 8,
                                    block * LANES : (block + 1) * LANES,
                                ]
        ok = usable[e].astype(jnp.float32)
        ok_last = jnp.where(low, ok, jnp.where(has_below, ok, 0.0))
        for which in (0, 1):
            def tap(ref, a):
                value = ref[e, a]
                return value * value if which else value

            filtered = tap(row_taps, 0) * raw[which, pl.ds(8 - radius, apart)]
            for a in range(1, taps):
                filtered += tap(row_taps, a) * raw[which, pl.ds(8 - radius + a, apart)]
            after, before = next_blocks(filtered), previous_blocks(filtered)
            result = tap(col_taps, radius) * filtered
            for d in range(1, radius + 1):
                right = pltpu.roll(choose(lane >= d, filtered, after), LANES - d, axis=2)
                left = pltpu.roll(choose(lane >= LANES - d, before, filtered), d, axis=2)
                result += tap(col_taps, radius + d) * right + tap(col_taps, radius - d) * left
            result = result.astype(jnp.bfloat16).astype(jnp.float32)
            inside = rows - apart
            result = jnp.concatenate([result[:inside] * ok, result[inside:] * ok_last], axis=0)
            step = apart - half
            table = jnp.concatenate(
                [
                    choose(low, result[:step], roll4(result[half:])),
                    choose(low, result[step:], result[:half]),
                    choose(low, roll4(result[:inside]), result[half : half + inside]),
                ],
                axis=0,
            )
            for copy, value in enumerate((previous_blocks(table), table, next_blocks(table))):
                maps[which, pl.ds(copy * span + e * rows, rows)] = value

        for velocity in range(vels):
            for which in (0, 1):
                for start in range(0, half, 8):
                    stacks[velocity, which, pl.ds(start, 8)] += window(e, velocity, which, start)

    def put(stage, g, v, start, signal, depth):
        for base, value in (
            (start, jnp.where(low, signal, roll4(depth))),
            (start + half, jnp.where(low, roll4(signal), depth)),
        ):
            for part in range(8 // own):
                owner = base // own + part
                sums[stage][g, owner % 2, owner // 2, v] = value[part * own : (part + 1) * own]

    def get_rows(g, start):
        return jnp.concatenate(
            [
                from_code(
                    fluxes[g, (start // own + part) % 2, (start // own + part) // 2], steps
                )
                for part in range(8 // own)
            ],
            axis=0,
        ).reshape(8, 8, LANES)

    def pass_on(stage, g):
        near_copy(stage, g).wait_recv()
        mine[stage][g] = sums[stage][g, core, chip] + near[stage][g, chip]
        for j in range(1, chips):
            there = peer(j)
            both = sums[stage][g, core, there] + near[stage][g, there]
            pair[stage][g, there] = to_code(both.reshape(2, own * 8, LANES), steps)
            far_copy(stage, g, j).start()

    def total(stage, g):
        value = mine[stage][g]
        for j in range(1, chips):
            far_copy(stage, g, j).wait_recv()
            value = value + from_code(far[stage][g, j - 1], steps).reshape(value.shape)
        return value

    @pl.loop(0, groups)
    def _(g):
        for v in (0, 1):
            for start in range(0, half, 8):
                put(
                    0, g, v, start,
                    stacks[2 * g + v, 0, pl.ds(start, 8)], stacks[2 * g + v, 1, pl.ds(start, 8)],
                )
        near_copy(0, g).start()

    @pl.loop(0, groups)
    def _(g):
        pass_on(0, g)

    def spread_flux(g):
        whole = total(0, g)
        flux = whole / (roll4(whole) + 1.0)
        flux = jnp.where(low, flux[0], roll4(flux[1])).reshape(own * 8, LANES)
        fluxes[g, core, chip] = to_code(flux, steps)
        for j in range(1, chips):
            flux_copy(g, j).start()

    def share_flux(g):
        for j in range(1, chips):
            flux_copy(g, j).wait_recv()
        flux_sibling(g).start()

    def reweight(g):
        flux_sibling(g).wait_recv()
        for start in range(0, half, 8):
            upper, lower = get_rows(g, start), get_rows(g, start + half)
            for v in (0, 1):
                if v == 0:
                    flux = jnp.where(low, upper, roll4(lower))
                else:
                    flux = jnp.where(low, roll4(upper), lower)
                signal_sum = jnp.zeros((8, 8, LANES), jnp.float32)
                depth_sum = jnp.zeros((8, 8, LANES), jnp.float32)
                for e in range(exposures):
                    signal = window(e, 2 * g + v, 0, start)
                    depth = window(e, 2 * g + v, 1, start)
                    residual = signal - flux * depth
                    more = depth + 1.0
                    bottom = more + residual * residual
                    guess = pl.reciprocal(bottom, approx=True)
                    weight = more * (guess * (2.0 - bottom * guess))
                    signal_sum += weight * signal
                    depth_sum += weight * depth
                put(1, g, v, start, signal_sum, depth_sum)
        near_copy(1, g).start()

    @pl.loop(0, groups)
    def _(g):
        spread_flux(g)

    @pl.loop(0, groups + 2)
    def _(i):
        @pl.when(i < groups)
        def _():
            share_flux(i)

        @pl.when((i >= 1) & (i < groups + 1))
        def _():
            reweight(i - 1)

        @pl.when(i >= 2)
        def _():
            pass_on(1, i - 2)

    @pl.loop(0, groups)
    def _(g):
        whole = total(1, g)
        result = whole / jnp.sqrt(roll4(whole) + 1.0)
        final[...] = result.reshape(2 * own * 8, LANES)
        for v in (0, 1):
            for block in range(blocks):
                out[2 * g + v, :, block * LANES : (block + 1) * LANES] = final[
                    pl.ds(v * own * 8 + block, own, stride=8), :
                ]

    @pl.loop(0, groups)
    def _(g):
        for stage in (0, 1):
            near_copy(stage, g).wait_send()
            for j in range(1, chips):
                far_copy(stage, g, j).wait_send()
        for j in range(1, chips):
            flux_copy(g, j).wait_send()
        flux_sibling(g).wait_send()

    @pl.when(has_below)
    def _():
        for t in range(tiles):
            for array in (0, 1):
                edge_copy(t, array, 1).wait_send()

    @pl.when(has_above)
    def _():
        for t in range(tiles):
            for array in (0, 1):
                edge_copy(t, array, 0).wait_send()

        @pl.loop(0, exposures)
        def _(e):
            for array in (0, 1):
                full_copy(e, array).wait_send()


def per_device(count, strips, science, inv_var, psf_rows, psf_cols, row_shift, col_shift, ok):
    exposures, rows, columns = science.shape
    vels, taps = row_shift.shape[1], psf_rows.shape[1]
    chips, own, groups = count // 2, rows // count, vels // 2
    f32, bf16 = jnp.float32, jnp.bfloat16
    dma = lambda *shape: [pltpu.SemaphoreType.DMA(shape)] * 2
    radius = taps // 2
    tiles = exposures * radius // 16
    stage = [
        pltpu.VMEM((groups, 2, chips, 2, own, 8, LANES), f32),
        pltpu.VMEM((groups, chips, 2, own, 8, LANES), f32),
        pltpu.VMEM((groups, 2, own, 8, LANES), f32),
        pltpu.VMEM((groups, chips, 2, own * 8, LANES), jnp.int16),
        pltpu.VMEM((groups, chips - 1, 2, own * 8, LANES), jnp.int16),
    ]
    result = pl.pallas_call(
        functools.partial(kernel, (count, strips, exposures, rows, columns, vels, taps)),
        out_shape=jax.ShapeDtypeStruct((vels, own, columns), f32),
        in_specs=[pl.BlockSpec(memory_space=pl.ANY)] * 7,
        out_specs=pl.BlockSpec(memory_space=pltpu.VMEM),
        scratch_shapes=[
            pltpu.SMEM(psf_rows.shape, f32),
            pltpu.SMEM(psf_cols.shape, f32),
            pltpu.SMEM(row_shift.shape, jnp.int32),
            pltpu.SMEM(col_shift.shape, jnp.int32),
            pltpu.SMEM(ok.shape, jnp.int32),
            pltpu.VMEM(science.shape, bf16),
            pltpu.VMEM(science.shape, bf16),
            pltpu.SemaphoreType.DMA((7,)),
            pltpu.VMEM((2, exposures, SHIFT, columns), bf16),
            pltpu.VMEM((2, tiles, 16, columns), bf16),
            pltpu.VMEM((2, tiles, 16, columns), bf16),
            pltpu.VMEM((2, 2, tiles, 16, columns), bf16),
            pltpu.VMEM((2, 2, 16 // radius, 8, columns), f32),
            pltpu.VMEM((2, (rows + SHIFT) // 2 + 16, 8, LANES), f32),
            pltpu.VMEM((2, 3 * exposures * rows, 8, LANES), f32),
            pltpu.VMEM((vels, 2, rows // 2, 8, LANES), f32),
            pltpu.VMEM((groups, 2, chips, own * 8, LANES), jnp.int16),
            pltpu.VMEM((2 * own * 8, LANES), f32),
            *stage,
            *stage,
            *dma(2, exposures),
            *dma(2, 2, tiles),
            *dma(2, groups),
            *dma(2, groups, chips - 1),
            *dma(groups, chips - 1),
            *dma(groups),
        ],
        compiler_params=pltpu.CompilerParams(
            collective_id=0, has_side_effects=True, vmem_limit_bytes=60 * 1024 * 1024
        ),
    )(psf_rows, psf_cols, row_shift, col_shift, ok, science, inv_var)
    return result.reshape(1, vels, own, columns)


def solution(mesh):
    from jax.sharding import PartitionSpec as P

    in_specs = (
        P(("field", "expo"), "strip", None),
        P(("field", "expo"), "strip", None),
        P(("field", "expo"), None),
        P(("field", "expo"), None),
        P(("field", "expo"), None),
        P(("field", "expo"), None),
        P(("field", "expo")),
    )
    return jax.shard_map(
        functools.partial(per_device, mesh.shape["expo"], mesh.shape["strip"]),
        mesh=mesh,
        in_specs=in_specs,
        out_specs=P("strip", "field", "expo", None),
        check_vma=False,
    )
```

```python
import functools
import math

import jax
import jax.numpy as jnp
from jax import lax
from jax.experimental import pallas as pl
from jax.experimental.pallas import tpu as pltpu

SHIFT = 16
LANES = 128
MESH = pl.DeviceIdType.MESH


LEAST = 2.0 ** -20
STEPS = 32700.0


def to_code(x, steps):
    level = jnp.log(1.0 + jnp.abs(x) * (1.0 / LEAST)) * steps + 0.5
    return jnp.where(x < 0, -level, level).astype(jnp.int32).astype(jnp.int16)


def from_code(code, steps):
    level = code.astype(jnp.int32).astype(jnp.float32)
    size = (jnp.exp(jnp.abs(level) * (1.0 / steps)) - 1.0) * LEAST
    return jnp.where(level < 0, -size, size)


def roll4(x):
    return pltpu.roll(x, 4, axis=x.ndim - 2)


def kernel(
    cfg,
    *refs,
):
    out, inputs, copied = refs[7], refs[:7], refs[8:15]
    row_taps, col_taps, row_shift, col_shift, usable, sci, inv = copied
    (in_s, below, tails, above, edge_out, edges, raw, maps, stacks, fluxes, final, *rest) = refs[15:]
    count, strips, exposures, rows, columns, vels, taps = cfg
    radius = taps // 2
    chips = count // 2
    own = rows // count
    half = rows // 2
    blocks = columns // LANES
    groups = vels // 2
    apart = (rows + SHIFT) // 2
    sums, near, mine, pair, far = zip(rest[0:5], rest[5:10])
    (full_s, full_r, edge_s, edge_r, near_s, near_r,
     far_s, far_r, flux_s, flux_r, fsib_s, fsib_r) = rest[10:]
    per_tile = 16 // radius
    most = 2.0 * exposures * 24.0 * taps * taps * 1.01
    steps = STEPS / math.log(1.0 + most / LEAST)
    tiles = exposures // per_tile

    me = lax.axis_index("expo")
    strip = lax.axis_index("strip")
    chip, core = me // 2, me % 2
    sibling = chip * 2 + (1 - core)
    has_above = strip > 0
    has_below = strip < strips - 1

    def peer(j):
        return (chip + j) % chips

    def full_copy(e, array):
        return pltpu.make_async_remote_copy(
            src_ref=inputs[5 + array].at[e, pl.ds(0, SHIFT)], dst_ref=below.at[array, e],
            send_sem=full_s.at[array, e], recv_sem=full_r.at[array, e],
            device_id={"strip": strip - 1}, device_id_type=MESH,
        )

    def edge_copy(t, array, down):
        return pltpu.make_async_remote_copy(
            src_ref=edge_out.at[down, array, t], dst_ref=(tails, above)[down].at[array, t],
            send_sem=edge_s.at[down, array, t], recv_sem=edge_r.at[down, array, t],
            device_id={"strip": strip + 1 if down else strip - 1}, device_id_type=MESH,
        )

    def near_copy(stage, g):
        return pltpu.make_async_remote_copy(
            src_ref=sums[stage].at[g, 1 - core], dst_ref=near[stage].at[g],
            send_sem=near_s.at[stage, g], recv_sem=near_r.at[stage, g],
            device_id={"expo": sibling}, device_id_type=MESH,
        )

    def far_copy(stage, g, j):
        return pltpu.make_async_remote_copy(
            src_ref=pair[stage].at[g, peer(j)], dst_ref=far[stage].at[g, j - 1],
            send_sem=far_s.at[stage, g, j - 1], recv_sem=far_r.at[stage, g, j - 1],
            device_id={"expo": peer(j) * 2 + core}, device_id_type=MESH,
        )

    def flux_copy(g, j):
        mine = fluxes.at[g, core, chip]
        return pltpu.make_async_remote_copy(
            src_ref=mine, dst_ref=mine,
            send_sem=flux_s.at[g, j - 1], recv_sem=flux_r.at[g, j - 1],
            device_id={"expo": peer(j) * 2 + core}, device_id_type=MESH,
        )

    def flux_sibling(g):
        mine = fluxes.at[g, core]
        return pltpu.make_async_remote_copy(
            src_ref=mine, dst_ref=mine, send_sem=fsib_s.at[g], recv_sem=fsib_r.at[g],
            device_id={"expo": sibling}, device_id_type=MESH,
        )

    local = [
        pltpu.make_async_copy(inputs[k], copied[k], in_s.at[k]) for k in (5, 6, 0, 1, 2, 3, 4)
    ]
    for copy in local:
        copy.start()
    barrier = pltpu.get_barrier_semaphore()
    pl.semaphore_signal(barrier, inc=1, device_id={"expo": sibling}, device_id_type=MESH)
    for j in range(1, chips):
        pl.semaphore_signal(
            barrier, inc=1, device_id={"expo": peer(j) * 2 + core}, device_id_type=MESH
        )

    @pl.when(has_above)
    def _():
        pl.semaphore_signal(barrier, inc=1, device_id={"strip": strip - 1}, device_id_type=MESH)

    @pl.when(has_below)
    def _():
        pl.semaphore_signal(barrier, inc=1, device_id={"strip": strip + 1}, device_id_type=MESH)

    pl.semaphore_wait(barrier, chips + has_above.astype(jnp.int32) + has_below.astype(jnp.int32))

    @pl.when(has_above)
    def _():
        for e in (0, 1):
            for array in (0, 1):
                full_copy(e, array).start()

    for copy in local[:2]:
        copy.wait()
    for array, source in enumerate((sci, inv)):
        for t in range(tiles):
            span = range(t * per_tile, (t + 1) * per_tile)
            for down, at in ((0, SHIFT), (1, rows - radius)):
                base = at // 16 * 16
                pieces = [
                    source[e, base : base + 16, :].astype(jnp.float32)[
                        at - base : at - base + radius
                    ]
                    for e in span
                ]
                edge_out[down, array, t] = jnp.concatenate(pieces, axis=0).astype(jnp.bfloat16)

    @pl.when(has_below)
    def _():
        for t in range(tiles):
            for array in (0, 1):
                edge_copy(t, array, 1).start()

    @pl.when(has_above)
    def _():
        @pl.loop(0, tiles)
        def _(t):
            for array in (0, 1):
                edge_copy(t, array, 0).start()

            @pl.loop(0, per_tile)
            def _(q):
                e = t * per_tile + q

                @pl.when(e > 1)
                def _():
                    for array in (0, 1):
                        full_copy(e, array).start()

    @pl.when(jnp.logical_not(has_above))
    def _():
        above[...] = jnp.zeros_like(above)

    @pl.when(jnp.logical_not(has_below))
    def _():
        below[...] = jnp.zeros_like(below)
        tails[...] = jnp.zeros_like(tails)

    stacks[...] = jnp.zeros_like(stacks)
    for copy in local[2:]:
        copy.wait()

    sub = lax.broadcasted_iota(jnp.int32, (1, 8, LANES), 1)
    lane = lax.broadcasted_iota(jnp.int32, (1, 8, LANES), 2)
    low = sub < 4
    first_block, last_block = sub % 4 == 0, sub % 4 == 3
    span = exposures * rows

    def choose(mask, x, y):
        return jnp.where(jnp.broadcast_to(mask, x.shape), x, y)

    def next_blocks(x):
        return choose(last_block, jnp.zeros_like(x), pltpu.roll(x, 7, axis=1))

    def previous_blocks(x):
        return choose(first_block, jnp.zeros_like(x), pltpu.roll(x, 1, axis=1))

    def window(e, velocity, which, start):
        shift = col_shift[e, velocity]
        left = jnp.where(shift < 0, 0, span) + e * rows + row_shift[e, velocity] + start
        here = maps[which, pl.ds(left, 8)]
        after = maps[which, pl.ds(left + span, 8)]
        mixed = choose(lane >= (shift & (LANES - 1)), here, after)
        return pltpu.roll(mixed, (-shift) & (LANES - 1), axis=2)

    raw_rows = raw.reshape(2, raw.shape[1] * 8, LANES)

    @pl.loop(0, exposures)
    def _(e):
        tile_now, place_in_tile = e // per_tile, e % per_tile

        @pl.when(place_in_tile == 0)
        def _():
            @pl.when(has_below)
            def _():
                for array in (0, 1):
                    edge_copy(tile_now, array, 0).wait_recv()

            @pl.when(has_above)
            def _():
                for array in (0, 1):
                    edge_copy(tile_now, array, 1).wait_recv()

            for down, source in enumerate((tails, above)):
                for array in (0, 1):
                    tile = source[array, tile_now].astype(jnp.float32)
                    for q in range(per_tile):
                        piece = tile[q * radius : (q + 1) * radius]
                        edges[down, array, q] = jnp.concatenate([piece] * (8 // radius), axis=0)

        @pl.when(has_below)
        def _():
            for array in (0, 1):
                full_copy(e, array).wait_recv()

        for first, pick in (
            (-8, lambda k: edges[1, k, place_in_tile]),
            *((r, lambda k, r=r: (sci, inv)[k][e, r : r + 16, :]) for r in range(0, rows, 16)),
            (rows, lambda k: below[k, e]),
            (rows + SHIFT, lambda k: edges[0, k, place_in_tile]),
        ):
            inverse = pick(1).astype(jnp.float32)
            weighted = pick(0).astype(jnp.float32) * inverse
            for which, value in enumerate((weighted, inverse)):
                for r in range(first, first + value.shape[0], 8):
                    for at, shift in ((r + 8, 0), (r + 8 - apart, 4)):
                        if 0 <= at <= apart + 8:
                            for block in range(blocks):
                                raw_rows[
                                    which, pl.ds(at * 8 + shift + block, 8, stride=8), :
                                ] = value[
                                    r - first : r - first + 8,
                                    block * LANES : (block + 1) * LANES,
                                ]
        ok = usable[e].astype(jnp.float32)
        ok_last = jnp.where(low, ok, jnp.where(has_below, ok, 0.0))
        for which in (0, 1):
            def tap(ref, a):
                value = ref[e, a]
                return value * value if which else value

            filtered = tap(row_taps, 0) * raw[which, pl.ds(8 - radius, apart)]
            for a in range(1, taps):
                filtered += tap(row_taps, a) * raw[which, pl.ds(8 - radius + a, apart)]
            after, before = next_blocks(filtered), previous_blocks(filtered)
            result = tap(col_taps, radius) * filtered
            for d in range(1, radius + 1):
                right = pltpu.roll(choose(lane >= d, filtered, after), LANES - d, axis=2)
                left = pltpu.roll(choose(lane >= LANES - d, before, filtered), d, axis=2)
                result += tap(col_taps, radius + d) * right + tap(col_taps, radius - d) * left
            result = result.astype(jnp.bfloat16).astype(jnp.float32)
            inside = rows - apart
            result = jnp.concatenate([result[:inside] * ok, result[inside:] * ok_last], axis=0)
            step = apart - half
            table = jnp.concatenate(
                [
                    choose(low, result[:step], roll4(result[half:])),
                    choose(low, result[step:], result[:half]),
                    choose(low, roll4(result[:inside]), result[half : half + inside]),
                ],
                axis=0,
            )
            for copy, value in enumerate((previous_blocks(table), table, next_blocks(table))):
                maps[which, pl.ds(copy * span + e * rows, rows)] = value

        for velocity in range(vels):
            for which in (0, 1):
                for start in range(0, half, 8):
                    stacks[velocity, which, pl.ds(start, 8)] += window(e, velocity, which, start)

    def put(stage, g, v, start, signal, depth):
        for base, value in (
            (start, jnp.where(low, signal, roll4(depth))),
            (start + half, jnp.where(low, roll4(signal), depth)),
        ):
            for part in range(8 // own):
                owner = base // own + part
                sums[stage][g, owner % 2, owner // 2, v] = value[part * own : (part + 1) * own]

    def get_rows(g, start):
        return jnp.concatenate(
            [
                from_code(
                    fluxes[g, (start // own + part) % 2, (start // own + part) // 2], steps
                )
                for part in range(8 // own)
            ],
            axis=0,
        ).reshape(8, 8, LANES)

    def pass_on(stage, g):
        near_copy(stage, g).wait_recv()
        mine[stage][g] = sums[stage][g, core, chip] + near[stage][g, chip]
        for j in range(1, chips):
            there = peer(j)
            both = sums[stage][g, core, there] + near[stage][g, there]
            pair[stage][g, there] = to_code(both.reshape(2, own * 8, LANES), steps)
            far_copy(stage, g, j).start()

    def total(stage, g):
        value = mine[stage][g]
        for j in range(1, chips):
            far_copy(stage, g, j).wait_recv()
            value = value + from_code(far[stage][g, j - 1], steps).reshape(value.shape)
        return value

    @pl.loop(0, groups)
    def _(g):
        for v in (0, 1):
            for start in range(0, half, 8):
                put(
                    0, g, v, start,
                    stacks[2 * g + v, 0, pl.ds(start, 8)], stacks[2 * g + v, 1, pl.ds(start, 8)],
                )
        near_copy(0, g).start()

    @pl.loop(0, groups)
    def _(g):
        pass_on(0, g)

    def spread_flux(g):
        whole = total(0, g)
        flux = whole / (roll4(whole) + 1.0)
        flux = jnp.where(low, flux[0], roll4(flux[1])).reshape(own * 8, LANES)
        fluxes[g, core, chip] = to_code(flux, steps)
        for j in range(1, chips):
            flux_copy(g, j).start()

    def share_flux(g):
        for j in range(1, chips):
            flux_copy(g, j).wait_recv()
        flux_sibling(g).start()

    def reweight(g):
        flux_sibling(g).wait_recv()
        for start in range(0, half, 8):
            upper, lower = get_rows(g, start), get_rows(g, start + half)
            for v in (0, 1):
                if v == 0:
                    flux = jnp.where(low, upper, roll4(lower))
                else:
                    flux = jnp.where(low, roll4(upper), lower)
                signal_sum = jnp.zeros((8, 8, LANES), jnp.float32)
                depth_sum = jnp.zeros((8, 8, LANES), jnp.float32)
                for e in range(exposures):
                    signal = window(e, 2 * g + v, 0, start)
                    depth = window(e, 2 * g + v, 1, start)
                    residual = signal - flux * depth
                    more = depth + 1.0
                    bottom = more + residual * residual
                    guess = pl.reciprocal(bottom, approx=True)
                    weight = more * (guess * (2.0 - bottom * guess))
                    signal_sum += weight * signal
                    depth_sum += weight * depth
                put(1, g, v, start, signal_sum, depth_sum)
        near_copy(1, g).start()

    @pl.loop(0, groups)
    def _(g):
        spread_flux(g)

    @pl.loop(0, groups + 2)
    def _(i):
        @pl.when(i < groups)
        def _():
            share_flux(i)

        @pl.when((i >= 1) & (i < groups + 1))
        def _():
            reweight(i - 1)

        @pl.when(i >= 2)
        def _():
            pass_on(1, i - 2)

    @pl.loop(0, groups)
    def _(g):
        whole = total(1, g)
        result = whole / jnp.sqrt(roll4(whole) + 1.0)
        final[...] = result.reshape(2 * own * 8, LANES)
        for v in (0, 1):
            for block in range(blocks):
                out[2 * g + v, :, block * LANES : (block + 1) * LANES] = final[
                    pl.ds(v * own * 8 + block, own, stride=8), :
                ]

    @pl.loop(0, groups)
    def _(g):
        for stage in (0, 1):
            near_copy(stage, g).wait_send()
            for j in range(1, chips):
                far_copy(stage, g, j).wait_send()
        for j in range(1, chips):
            flux_copy(g, j).wait_send()
        flux_sibling(g).wait_send()

    @pl.when(has_below)
    def _():
        for t in range(tiles):
            for array in (0, 1):
                edge_copy(t, array, 1).wait_send()

    @pl.when(has_above)
    def _():
        for t in range(tiles):
            for array in (0, 1):
                edge_copy(t, array, 0).wait_send()

        @pl.loop(0, exposures)
        def _(e):
            for array in (0, 1):
                full_copy(e, array).wait_send()


def per_device(count, strips, science, inv_var, psf_rows, psf_cols, row_shift, col_shift, ok):
    exposures, rows, columns = science.shape
    vels, taps = row_shift.shape[1], psf_rows.shape[1]
    chips, own, groups = count // 2, rows // count, vels // 2
    f32, bf16 = jnp.float32, jnp.bfloat16
    dma = lambda *shape: [pltpu.SemaphoreType.DMA(shape)] * 2
    radius = taps // 2
    tiles = exposures * radius // 16
    stage = [
        pltpu.VMEM((groups, 2, chips, 2, own, 8, LANES), f32),
        pltpu.VMEM((groups, chips, 2, own, 8, LANES), f32),
        pltpu.VMEM((groups, 2, own, 8, LANES), f32),
        pltpu.VMEM((groups, chips, 2, own * 8, LANES), jnp.int16),
        pltpu.VMEM((groups, chips - 1, 2, own * 8, LANES), jnp.int16),
    ]
    result = pl.pallas_call(
        functools.partial(kernel, (count, strips, exposures, rows, columns, vels, taps)),
        out_shape=jax.ShapeDtypeStruct((vels, own, columns), f32),
        in_specs=[pl.BlockSpec(memory_space=pl.ANY)] * 7,
        out_specs=pl.BlockSpec(memory_space=pltpu.VMEM),
        scratch_shapes=[
            pltpu.SMEM(psf_rows.shape, f32),
            pltpu.SMEM(psf_cols.shape, f32),
            pltpu.SMEM(row_shift.shape, jnp.int32),
            pltpu.SMEM(col_shift.shape, jnp.int32),
            pltpu.SMEM(ok.shape, jnp.int32),
            pltpu.VMEM(science.shape, bf16),
            pltpu.VMEM(science.shape, bf16),
            pltpu.SemaphoreType.DMA((7,)),
            pltpu.VMEM((2, exposures, SHIFT, columns), bf16),
            pltpu.VMEM((2, tiles, 16, columns), bf16),
            pltpu.VMEM((2, tiles, 16, columns), bf16),
            pltpu.VMEM((2, 2, tiles, 16, columns), bf16),
            pltpu.VMEM((2, 2, 16 // radius, 8, columns), f32),
            pltpu.VMEM((2, (rows + SHIFT) // 2 + 16, 8, LANES), f32),
            pltpu.VMEM((2, 3 * exposures * rows, 8, LANES), f32),
            pltpu.VMEM((vels, 2, rows // 2, 8, LANES), f32),
            pltpu.VMEM((groups, 2, chips, own * 8, LANES), jnp.int16),
            pltpu.VMEM((2 * own * 8, LANES), f32),
            *stage,
            *stage,
            *dma(2, exposures),
            *dma(2, 2, tiles),
            *dma(2, groups),
            *dma(2, groups, chips - 1),
            *dma(groups, chips - 1),
            *dma(groups),
        ],
        compiler_params=pltpu.CompilerParams(
            collective_id=0, has_side_effects=True, vmem_limit_bytes=24 * 1024 * 1024
        ),
    )(
        *(
            pltpu.with_memory_space_constraint(x, pltpu.HBM)
            for x in (psf_rows, psf_cols, row_shift, col_shift, ok, science, inv_var)
        )
    )
    return result.reshape(1, vels, own, columns)


def solution(mesh):
    from jax.sharding import PartitionSpec as P

    in_specs = (
        P(("field", "expo"), "strip", None),
        P(("field", "expo"), "strip", None),
        P(("field", "expo"), None),
        P(("field", "expo"), None),
        P(("field", "expo"), None),
        P(("field", "expo"), None),
        P(("field", "expo")),
    )
    return jax.shard_map(
        functools.partial(per_device, mesh.shape["expo"], mesh.shape["strip"]),
        mesh=mesh,
        in_specs=in_specs,
        out_specs=P("strip", "field", "expo", None),
        check_vma=False,
    )
```

```python
import functools
import math

import jax
import jax.numpy as jnp
from jax import lax
from jax.experimental import pallas as pl
from jax.experimental.pallas import tpu as pltpu

SHIFT = 16
LANES = 128
MESH = pl.DeviceIdType.MESH


LEAST = 2.0 ** -20
STEPS = 32700.0


def to_code(x, steps):
    level = jnp.log(1.0 + jnp.abs(x) * (1.0 / LEAST)) * steps + 0.5
    return jnp.where(x < 0, -level, level).astype(jnp.int32).astype(jnp.int16)


def from_code(code, steps):
    level = code.astype(jnp.int32).astype(jnp.float32)
    size = (jnp.exp(jnp.abs(level) * (1.0 / steps)) - 1.0) * LEAST
    return jnp.where(level < 0, -size, size)


def roll4(x):
    return pltpu.roll(x, 4, axis=x.ndim - 2)


def kernel(
    cfg,
    *refs,
):
    out, inputs, copied = refs[7], refs[:7], refs[8:15]
    row_taps, col_taps, row_shift, col_shift, usable, sci, inv = copied
    (in_s, below, tails, above, edge_out, edges, raw, maps, stacks, fluxes, final, *rest) = refs[15:]
    count, strips, exposures, rows, columns, vels, taps = cfg
    radius = taps // 2
    chips = count // 2
    own = rows // count
    half = rows // 2
    blocks = columns // LANES
    groups = vels // 2
    apart = (rows + SHIFT) // 2
    sums, near, mine, pair, far = zip(rest[0:5], rest[5:10])
    (full_s, full_r, edge_s, edge_r, near_s, near_r,
     far_s, far_r, flux_s, flux_r, fsib_s, fsib_r) = rest[10:]
    per_tile = 16 // radius
    most = 2.0 * exposures * 24.0 * taps * taps * 1.01
    steps = STEPS / math.log(1.0 + most / LEAST)
    tiles = exposures // per_tile

    me = lax.axis_index("expo")
    strip = lax.axis_index("strip")
    chip, core = me // 2, me % 2
    sibling = chip * 2 + (1 - core)
    has_above = strip > 0
    has_below = strip < strips - 1

    others = sorted(range(1, chips), key=lambda j: -min(j, chips - j))

    def peer(j):
        return (chip + j) % chips

    def full_copy(e, array):
        return pltpu.make_async_remote_copy(
            src_ref=inputs[5 + array].at[e, pl.ds(0, SHIFT)], dst_ref=below.at[array, e],
            send_sem=full_s.at[array, e], recv_sem=full_r.at[array, e],
            device_id={"strip": strip - 1}, device_id_type=MESH,
        )

    def edge_copy(t, array, down):
        return pltpu.make_async_remote_copy(
            src_ref=edge_out.at[down, array, t], dst_ref=(tails, above)[down].at[array, t],
            send_sem=edge_s.at[down, array, t], recv_sem=edge_r.at[down, array, t],
            device_id={"strip": strip + 1 if down else strip - 1}, device_id_type=MESH,
        )

    def near_copy(stage, g):
        return pltpu.make_async_remote_copy(
            src_ref=sums[stage].at[g, 1 - core], dst_ref=near[stage].at[g],
            send_sem=near_s.at[stage, g], recv_sem=near_r.at[stage, g],
            device_id={"expo": sibling}, device_id_type=MESH,
        )

    def far_copy(stage, g, j):
        return pltpu.make_async_remote_copy(
            src_ref=pair[stage].at[g, peer(j)], dst_ref=far[stage].at[g, j - 1],
            send_sem=far_s.at[stage, g, j - 1], recv_sem=far_r.at[stage, g, j - 1],
            device_id={"expo": peer(j) * 2 + core}, device_id_type=MESH,
        )

    def flux_copy(g, j):
        mine = fluxes.at[g, core, chip]
        return pltpu.make_async_remote_copy(
            src_ref=mine, dst_ref=mine,
            send_sem=flux_s.at[g, j - 1], recv_sem=flux_r.at[g, j - 1],
            device_id={"expo": peer(j) * 2 + core}, device_id_type=MESH,
        )

    def flux_sibling(g):
        mine = fluxes.at[g, core]
        return pltpu.make_async_remote_copy(
            src_ref=mine, dst_ref=mine, send_sem=fsib_s.at[g], recv_sem=fsib_r.at[g],
            device_id={"expo": sibling}, device_id_type=MESH,
        )

    local = [
        pltpu.make_async_copy(inputs[k], copied[k], in_s.at[k]) for k in (5, 6, 0, 1, 2, 3, 4)
    ]
    for copy in local:
        copy.start()
    barrier = pltpu.get_barrier_semaphore()
    pl.semaphore_signal(barrier, inc=1, device_id={"expo": sibling}, device_id_type=MESH)
    for j in others:
        pl.semaphore_signal(
            barrier, inc=1, device_id={"expo": peer(j) * 2 + core}, device_id_type=MESH
        )

    @pl.when(has_above)
    def _():
        pl.semaphore_signal(barrier, inc=1, device_id={"strip": strip - 1}, device_id_type=MESH)

    @pl.when(has_below)
    def _():
        pl.semaphore_signal(barrier, inc=1, device_id={"strip": strip + 1}, device_id_type=MESH)

    pl.semaphore_wait(barrier, chips + has_above.astype(jnp.int32) + has_below.astype(jnp.int32))

    @pl.when(has_above)
    def _():
        for e in (0, 1):
            for array in (0, 1):
                full_copy(e, array).start()

    for copy in local[:2]:
        copy.wait()
    for array, source in enumerate((sci, inv)):
        for t in range(tiles):
            span = range(t * per_tile, (t + 1) * per_tile)
            for down, at in ((0, SHIFT), (1, rows - radius)):
                base = at // 16 * 16
                pieces = [
                    source[e, base : base + 16, :].astype(jnp.float32)[
                        at - base : at - base + radius
                    ]
                    for e in span
                ]
                edge_out[down, array, t] = jnp.concatenate(pieces, axis=0).astype(jnp.bfloat16)

    @pl.when(has_below)
    def _():
        for t in range(tiles):
            for array in (0, 1):
                edge_copy(t, array, 1).start()

    @pl.when(has_above)
    def _():
        @pl.loop(0, tiles)
        def _(t):
            for array in (0, 1):
                edge_copy(t, array, 0).start()

            @pl.loop(0, per_tile)
            def _(q):
                e = t * per_tile + q

                @pl.when(e > 1)
                def _():
                    for array in (0, 1):
                        full_copy(e, array).start()

    @pl.when(jnp.logical_not(has_above))
    def _():
        above[...] = jnp.zeros_like(above)

    @pl.when(jnp.logical_not(has_below))
    def _():
        below[...] = jnp.zeros_like(below)
        tails[...] = jnp.zeros_like(tails)

    stacks[...] = jnp.zeros_like(stacks)
    for copy in local[2:]:
        copy.wait()

    sub = lax.broadcasted_iota(jnp.int32, (1, 8, LANES), 1)
    lane = lax.broadcasted_iota(jnp.int32, (1, 8, LANES), 2)
    low = sub < 4
    first_block, last_block = sub % 4 == 0, sub % 4 == 3
    span = exposures * rows

    def choose(mask, x, y):
        return jnp.where(jnp.broadcast_to(mask, x.shape), x, y)

    def next_blocks(x):
        return choose(last_block, jnp.zeros_like(x), pltpu.roll(x, 7, axis=1))

    def previous_blocks(x):
        return choose(first_block, jnp.zeros_like(x), pltpu.roll(x, 1, axis=1))

    def window(e, velocity, which, start):
        shift = col_shift[e, velocity]
        left = jnp.where(shift < 0, 0, span) + e * rows + row_shift[e, velocity] + start
        here = maps[which, pl.ds(left, 8)]
        after = maps[which, pl.ds(left + span, 8)]
        mixed = choose(lane >= (shift & (LANES - 1)), here, after)
        return pltpu.roll(mixed, (-shift) & (LANES - 1), axis=2)

    raw_rows = raw.reshape(2, raw.shape[1] * 8, LANES)

    @pl.loop(0, exposures)
    def _(e):
        tile_now, place_in_tile = e // per_tile, e % per_tile

        @pl.when(place_in_tile == 0)
        def _():
            @pl.when(has_below)
            def _():
                for array in (0, 1):
                    edge_copy(tile_now, array, 0).wait_recv()

            @pl.when(has_above)
            def _():
                for array in (0, 1):
                    edge_copy(tile_now, array, 1).wait_recv()

            for down, source in enumerate((tails, above)):
                for array in (0, 1):
                    tile = source[array, tile_now].astype(jnp.float32)
                    for q in range(per_tile):
                        piece = tile[q * radius : (q + 1) * radius]
                        edges[down, array, q] = jnp.concatenate([piece] * (8 // radius), axis=0)

        @pl.when(has_below)
        def _():
            for array in (0, 1):
                full_copy(e, array).wait_recv()

        for first, pick in (
            (-8, lambda k: edges[1, k, place_in_tile]),
            *((r, lambda k, r=r: (sci, inv)[k][e, r : r + 16, :]) for r in range(0, rows, 16)),
            (rows, lambda k: below[k, e]),
            (rows + SHIFT, lambda k: edges[0, k, place_in_tile]),
        ):
            inverse = pick(1).astype(jnp.float32)
            weighted = pick(0).astype(jnp.float32) * inverse
            for which, value in enumerate((weighted, inverse)):
                for r in range(first, first + value.shape[0], 8):
                    for at, shift in ((r + 8, 0), (r + 8 - apart, 4)):
                        if 0 <= at <= apart + 8:
                            for block in range(blocks):
                                raw_rows[
                                    which, pl.ds(at * 8 + shift + block, 8, stride=8), :
                                ] = value[
                                    r - first : r - first + 8,
                                    block * LANES : (block + 1) * LANES,
                                ]
        ok = usable[e].astype(jnp.float32)
        ok_last = jnp.where(low, ok, jnp.where(has_below, ok, 0.0))
        for which in (0, 1):
            def tap(ref, a):
                value = ref[e, a]
                return value * value if which else value

            filtered = tap(row_taps, 0) * raw[which, pl.ds(8 - radius, apart)]
            for a in range(1, taps):
                filtered += tap(row_taps, a) * raw[which, pl.ds(8 - radius + a, apart)]
            after, before = next_blocks(filtered), previous_blocks(filtered)
            result = tap(col_taps, radius) * filtered
            for d in range(1, radius + 1):
                right = pltpu.roll(choose(lane >= d, filtered, after), LANES - d, axis=2)
                left = pltpu.roll(choose(lane >= LANES - d, before, filtered), d, axis=2)
                result += tap(col_taps, radius + d) * right + tap(col_taps, radius - d) * left
            result = result.astype(jnp.bfloat16).astype(jnp.float32)
            inside = rows - apart
            result = jnp.concatenate([result[:inside] * ok, result[inside:] * ok_last], axis=0)
            step = apart - half
            table = jnp.concatenate(
                [
                    choose(low, result[:step], roll4(result[half:])),
                    choose(low, result[step:], result[:half]),
                    choose(low, roll4(result[:inside]), result[half : half + inside]),
                ],
                axis=0,
            )
            for copy, value in enumerate((previous_blocks(table), table, next_blocks(table))):
                maps[which, pl.ds(copy * span + e * rows, rows)] = value

        @pl.when(e < exposures - 1)
        def _():
            for velocity in range(vels):
                for which in (0, 1):
                    for start in range(0, half, 8):
                        place = velocity, which, pl.ds(start, 8)
                        stacks[place] += window(e, velocity, which, start)

    def put(stage, g, v, start, signal, depth):
        for base, value in (
            (start, jnp.where(low, signal, roll4(depth))),
            (start + half, jnp.where(low, roll4(signal), depth)),
        ):
            for part in range(8 // own):
                owner = base // own + part
                sums[stage][g, owner % 2, owner // 2, v] = value[part * own : (part + 1) * own]

    def get_rows(g, start):
        return jnp.concatenate(
            [
                from_code(
                    fluxes[g, (start // own + part) % 2, (start // own + part) // 2], steps
                )
                for part in range(8 // own)
            ],
            axis=0,
        ).reshape(8, 8, LANES)

    def pass_on(stage, g):
        near_copy(stage, g).wait_recv()
        mine[stage][g] = sums[stage][g, core, chip] + near[stage][g, chip]
        for j in others:
            there = peer(j)
            both = sums[stage][g, core, there] + near[stage][g, there]
            pair[stage][g, there] = to_code(both.reshape(2, own * 8, LANES), steps)
            far_copy(stage, g, j).start()

    def total(stage, g):
        value = mine[stage][g]
        for j in others:
            far_copy(stage, g, j).wait_recv()
            value = value + from_code(far[stage][g, j - 1], steps).reshape(value.shape)
        return value

    @pl.loop(0, groups)
    def _(g):
        for v in (0, 1):
            for start in range(0, half, 8):
                signal, depth = (
                    stacks[2 * g + v, which, pl.ds(start, 8)]
                    + window(exposures - 1, 2 * g + v, which, start)
                    for which in (0, 1)
                )
                put(0, g, v, start, signal, depth)
        near_copy(0, g).start()

    @pl.loop(0, groups)
    def _(g):
        pass_on(0, g)

    def spread_flux(g):
        whole = total(0, g)
        flux = whole / (roll4(whole) + 1.0)
        flux = jnp.where(low, flux[0], roll4(flux[1])).reshape(own * 8, LANES)
        fluxes[g, core, chip] = to_code(flux, steps)
        for j in others:
            flux_copy(g, j).start()

    def share_flux(g):
        for j in others:
            flux_copy(g, j).wait_recv()
        flux_sibling(g).start()

    def reweight(g):
        flux_sibling(g).wait_recv()
        for start in range(0, half, 8):
            upper, lower = get_rows(g, start), get_rows(g, start + half)
            for v in (0, 1):
                if v == 0:
                    flux = jnp.where(low, upper, roll4(lower))
                else:
                    flux = jnp.where(low, roll4(upper), lower)
                signal_sum = jnp.zeros((8, 8, LANES), jnp.float32)
                depth_sum = jnp.zeros((8, 8, LANES), jnp.float32)
                for e in range(exposures):
                    signal = window(e, 2 * g + v, 0, start)
                    depth = window(e, 2 * g + v, 1, start)
                    residual = signal - flux * depth
                    more = depth + 1.0
                    bottom = more + residual * residual
                    guess = pl.reciprocal(bottom, approx=True)
                    weight = more * (guess * (2.0 - bottom * guess))
                    signal_sum += weight * signal
                    depth_sum += weight * depth
                put(1, g, v, start, signal_sum, depth_sum)
        near_copy(1, g).start()

    @pl.loop(0, groups)
    def _(g):
        spread_flux(g)

    @pl.loop(0, groups + 2)
    def _(i):
        @pl.when(i < groups)
        def _():
            share_flux(i)

        @pl.when((i >= 1) & (i < groups + 1))
        def _():
            reweight(i - 1)

        @pl.when(i >= 2)
        def _():
            pass_on(1, i - 2)

    @pl.loop(0, groups)
    def _(g):
        whole = total(1, g)
        result = whole / jnp.sqrt(roll4(whole) + 1.0)
        final[...] = result.reshape(2 * own * 8, LANES)
        for v in (0, 1):
            for block in range(blocks):
                out[2 * g + v, :, block * LANES : (block + 1) * LANES] = final[
                    pl.ds(v * own * 8 + block, own, stride=8), :
                ]

    @pl.loop(0, groups)
    def _(g):
        for stage in (0, 1):
            near_copy(stage, g).wait_send()
            for j in others:
                far_copy(stage, g, j).wait_send()
        for j in others:
            flux_copy(g, j).wait_send()
        flux_sibling(g).wait_send()

    @pl.when(has_below)
    def _():
        for t in range(tiles):
            for array in (0, 1):
                edge_copy(t, array, 1).wait_send()

    @pl.when(has_above)
    def _():
        for t in range(tiles):
            for array in (0, 1):
                edge_copy(t, array, 0).wait_send()

        @pl.loop(0, exposures)
        def _(e):
            for array in (0, 1):
                full_copy(e, array).wait_send()


def per_device(count, strips, science, inv_var, psf_rows, psf_cols, row_shift, col_shift, ok):
    exposures, rows, columns = science.shape
    vels, taps = row_shift.shape[1], psf_rows.shape[1]
    chips, own, groups = count // 2, rows // count, vels // 2
    f32, bf16 = jnp.float32, jnp.bfloat16
    dma = lambda *shape: [pltpu.SemaphoreType.DMA(shape)] * 2
    radius = taps // 2
    tiles = exposures * radius // 16
    stage = [
        pltpu.VMEM((groups, 2, chips, 2, own, 8, LANES), f32),
        pltpu.VMEM((groups, chips, 2, own, 8, LANES), f32),
        pltpu.VMEM((groups, 2, own, 8, LANES), f32),
        pltpu.VMEM((groups, chips, 2, own * 8, LANES), jnp.int16),
        pltpu.VMEM((groups, chips - 1, 2, own * 8, LANES), jnp.int16),
    ]
    result = pl.pallas_call(
        functools.partial(kernel, (count, strips, exposures, rows, columns, vels, taps)),
        out_shape=jax.ShapeDtypeStruct((vels, own, columns), f32),
        in_specs=[pl.BlockSpec(memory_space=pl.ANY)] * 7,
        out_specs=pl.BlockSpec(memory_space=pltpu.VMEM),
        scratch_shapes=[
            pltpu.SMEM(psf_rows.shape, f32),
            pltpu.SMEM(psf_cols.shape, f32),
            pltpu.SMEM(row_shift.shape, jnp.int32),
            pltpu.SMEM(col_shift.shape, jnp.int32),
            pltpu.SMEM(ok.shape, jnp.int32),
            pltpu.VMEM(science.shape, bf16),
            pltpu.VMEM(science.shape, bf16),
            pltpu.SemaphoreType.DMA((7,)),
            pltpu.VMEM((2, exposures, SHIFT, columns), bf16),
            pltpu.VMEM((2, tiles, 16, columns), bf16),
            pltpu.VMEM((2, tiles, 16, columns), bf16),
            pltpu.VMEM((2, 2, tiles, 16, columns), bf16),
            pltpu.VMEM((2, 2, 16 // radius, 8, columns), f32),
            pltpu.VMEM((2, (rows + SHIFT) // 2 + 16, 8, LANES), f32),
            pltpu.VMEM((2, 3 * exposures * rows, 8, LANES), f32),
            pltpu.VMEM((vels, 2, rows // 2, 8, LANES), f32),
            pltpu.VMEM((groups, 2, chips, own * 8, LANES), jnp.int16),
            pltpu.VMEM((2 * own * 8, LANES), f32),
            *stage,
            *stage,
            *dma(2, exposures),
            *dma(2, 2, tiles),
            *dma(2, groups),
            *dma(2, groups, chips - 1),
            *dma(groups, chips - 1),
            *dma(groups),
        ],
        compiler_params=pltpu.CompilerParams(
            collective_id=0, has_side_effects=True, vmem_limit_bytes=24 * 1024 * 1024
        ),
    )(
        *(
            pltpu.with_memory_space_constraint(x, pltpu.HBM)
            for x in (psf_rows, psf_cols, row_shift, col_shift, ok, science, inv_var)
        )
    )
    return result.reshape(1, vels, own, columns)


def solution(mesh):
    from jax.sharding import PartitionSpec as P

    in_specs = (
        P(("field", "expo"), "strip", None),
        P(("field", "expo"), "strip", None),
        P(("field", "expo"), None),
        P(("field", "expo"), None),
        P(("field", "expo"), None),
        P(("field", "expo"), None),
        P(("field", "expo")),
    )
    return jax.shard_map(
        functools.partial(per_device, mesh.shape["expo"], mesh.shape["strip"]),
        mesh=mesh,
        in_specs=in_specs,
        out_specs=P("strip", "field", "expo", None),
        check_vma=False,
    )
```

```python
import functools
import math

import jax
import jax.numpy as jnp
from jax import lax
from jax.experimental import pallas as pl
from jax.experimental.pallas import tpu as pltpu

SHIFT = 16
LANES = 128
MESH = pl.DeviceIdType.MESH


LEAST = 2.0 ** -20
STEPS = 32700.0


def to_code(x, steps):
    level = jnp.log(1.0 + jnp.abs(x) * (1.0 / LEAST)) * steps + 0.5
    return jnp.where(x < 0, -level, level).astype(jnp.int32).astype(jnp.int16)


def from_code(code, steps):
    level = code.astype(jnp.int32).astype(jnp.float32)
    size = (jnp.exp(jnp.abs(level) * (1.0 / steps)) - 1.0) * LEAST
    return jnp.where(level < 0, -size, size)


def roll4(x):
    return pltpu.roll(x, 4, axis=x.ndim - 2)


def kernel(
    cfg,
    *refs,
):
    out, inputs, copied = refs[7], refs[:7], refs[8:15]
    row_taps, col_taps, row_shift, col_shift, usable, sci, inv = copied
    (in_s, below, tails, above, edge_out, edges, raw, maps, stacks, fluxes, final, *rest) = refs[15:]
    count, strips, exposures, rows, columns, vels, taps = cfg
    radius = taps // 2
    chips = count // 2
    own = rows // count
    half = rows // 2
    blocks = columns // LANES
    groups = vels // 2
    apart = (rows + SHIFT) // 2
    sums, near, mine, pair, far = zip(rest[0:5], rest[5:10])
    (full_s, full_r, edge_s, edge_r, near_s, near_r,
     far_s, far_r, flux_s, flux_r, fsib_s, fsib_r) = rest[10:]
    per_tile = 16 // radius
    most = 2.0 * exposures * 24.0 * taps * taps * 1.01
    steps = STEPS / math.log(1.0 + most / LEAST)
    tiles = exposures // per_tile

    me = lax.axis_index("expo")
    strip = lax.axis_index("strip")
    chip, core = me // 2, me % 2
    sibling = chip * 2 + (1 - core)
    has_above = strip > 0
    has_below = strip < strips - 1

    others = sorted(range(1, chips), key=lambda j: -min(j, chips - j))

    def peer(j):
        return (chip + j) % chips

    def full_copy(e, array):
        return pltpu.make_async_remote_copy(
            src_ref=inputs[5 + array].at[e, pl.ds(0, SHIFT)], dst_ref=below.at[array, e],
            send_sem=full_s.at[array, e], recv_sem=full_r.at[array, e],
            device_id={"strip": strip - 1}, device_id_type=MESH,
        )

    def edge_copy(t, array, down):
        return pltpu.make_async_remote_copy(
            src_ref=edge_out.at[down, array, t], dst_ref=(tails, above)[down].at[array, t],
            send_sem=edge_s.at[down, array, t], recv_sem=edge_r.at[down, array, t],
            device_id={"strip": strip + 1 if down else strip - 1}, device_id_type=MESH,
        )

    def near_copy(stage, g):
        return pltpu.make_async_remote_copy(
            src_ref=sums[stage].at[g, 1 - core], dst_ref=near[stage].at[g],
            send_sem=near_s.at[stage, g], recv_sem=near_r.at[stage, g],
            device_id={"expo": sibling}, device_id_type=MESH,
        )

    def far_copy(stage, g, j):
        return pltpu.make_async_remote_copy(
            src_ref=pair[stage].at[g, peer(j)], dst_ref=far[stage].at[g, j - 1],
            send_sem=far_s.at[stage, g, j - 1], recv_sem=far_r.at[stage, g, j - 1],
            device_id={"expo": peer(j) * 2 + core}, device_id_type=MESH,
        )

    def flux_copy(g, j):
        mine = fluxes.at[g, core, chip]
        return pltpu.make_async_remote_copy(
            src_ref=mine, dst_ref=mine,
            send_sem=flux_s.at[g, j - 1], recv_sem=flux_r.at[g, j - 1],
            device_id={"expo": peer(j) * 2 + core}, device_id_type=MESH,
        )

    def flux_sibling(g):
        mine = fluxes.at[g, core]
        return pltpu.make_async_remote_copy(
            src_ref=mine, dst_ref=mine, send_sem=fsib_s.at[g], recv_sem=fsib_r.at[g],
            device_id={"expo": sibling}, device_id_type=MESH,
        )

    local = [
        pltpu.make_async_copy(inputs[k], copied[k], in_s.at[k]) for k in (5, 6, 0, 1, 2, 3, 4)
    ]
    for copy in local:
        copy.start()
    barrier = pltpu.get_barrier_semaphore()
    pl.semaphore_signal(barrier, inc=1, device_id={"expo": sibling}, device_id_type=MESH)
    for j in others:
        pl.semaphore_signal(
            barrier, inc=1, device_id={"expo": peer(j) * 2 + core}, device_id_type=MESH
        )

    @pl.when(has_above)
    def _():
        pl.semaphore_signal(barrier, inc=1, device_id={"strip": strip - 1}, device_id_type=MESH)

    @pl.when(has_below)
    def _():
        pl.semaphore_signal(barrier, inc=1, device_id={"strip": strip + 1}, device_id_type=MESH)

    pl.semaphore_wait(barrier, chips + has_above.astype(jnp.int32) + has_below.astype(jnp.int32))

    @pl.when(has_above)
    def _():
        for e in (0, 1):
            for array in (0, 1):
                full_copy(e, array).start()

    for copy in local[:2]:
        copy.wait()
    for array, source in enumerate((sci, inv)):
        for t in range(tiles):
            span = range(t * per_tile, (t + 1) * per_tile)
            for down, at in ((0, SHIFT), (1, rows - radius)):
                base = at // 16 * 16
                pieces = [
                    source[e, base : base + 16, :].astype(jnp.float32)[
                        at - base : at - base + radius
                    ]
                    for e in span
                ]
                edge_out[down, array, t] = jnp.concatenate(pieces, axis=0).astype(jnp.bfloat16)

    @pl.when(has_below)
    def _():
        for t in range(tiles):
            for array in (0, 1):
                edge_copy(t, array, 1).start()

    @pl.when(has_above)
    def _():
        @pl.loop(0, tiles)
        def _(t):
            for array in (0, 1):
                edge_copy(t, array, 0).start()

            @pl.loop(0, per_tile)
            def _(q):
                e = t * per_tile + q

                @pl.when(e > 1)
                def _():
                    for array in (0, 1):
                        full_copy(e, array).start()

    @pl.when(jnp.logical_not(has_above))
    def _():
        above[...] = jnp.zeros_like(above)

    @pl.when(jnp.logical_not(has_below))
    def _():
        below[...] = jnp.zeros_like(below)
        tails[...] = jnp.zeros_like(tails)

    stacks[...] = jnp.zeros_like(stacks)
    for copy in local[2:]:
        copy.wait()

    sub = lax.broadcasted_iota(jnp.int32, (1, 8, LANES), 1)
    lane = lax.broadcasted_iota(jnp.int32, (1, 8, LANES), 2)
    low = sub < 4
    first_block, last_block = sub % 4 == 0, sub % 4 == 3
    span = exposures * rows

    def choose(mask, x, y):
        return jnp.where(jnp.broadcast_to(mask, x.shape), x, y)

    def next_blocks(x):
        return choose(last_block, jnp.zeros_like(x), pltpu.roll(x, 7, axis=1))

    def previous_blocks(x):
        return choose(first_block, jnp.zeros_like(x), pltpu.roll(x, 1, axis=1))

    def window(e, velocity, which, start):
        shift = col_shift[e, velocity]
        left = jnp.where(shift < 0, 0, span) + e * rows + row_shift[e, velocity] + start
        here = maps[which, pl.ds(left, 8)]
        after = maps[which, pl.ds(left + span, 8)]
        mixed = choose(lane >= (shift & (LANES - 1)), here, after)
        return pltpu.roll(mixed, (-shift) & (LANES - 1), axis=2)

    raw_rows = raw.reshape(2, raw.shape[1] * 8, LANES)

    @pl.loop(0, exposures)
    def _(e):
        tile_now, place_in_tile = e // per_tile, e % per_tile

        @pl.when(place_in_tile == 0)
        def _():
            @pl.when(has_below)
            def _():
                for array in (0, 1):
                    edge_copy(tile_now, array, 0).wait_recv()

            @pl.when(has_above)
            def _():
                for array in (0, 1):
                    edge_copy(tile_now, array, 1).wait_recv()

            for down, source in enumerate((tails, above)):
                for array in (0, 1):
                    tile = source[array, tile_now].astype(jnp.float32)
                    for q in range(per_tile):
                        piece = tile[q * radius : (q + 1) * radius]
                        edges[down, array, q] = jnp.concatenate([piece] * (8 // radius), axis=0)

        @pl.when(has_below)
        def _():
            for array in (0, 1):
                full_copy(e, array).wait_recv()

        for first, pick in (
            (-8, lambda k: edges[1, k, place_in_tile]),
            *((r, lambda k, r=r: (sci, inv)[k][e, r : r + 16, :]) for r in range(0, rows, 16)),
            (rows, lambda k: below[k, e]),
            (rows + SHIFT, lambda k: edges[0, k, place_in_tile]),
        ):
            inverse = pick(1).astype(jnp.float32)
            weighted = pick(0).astype(jnp.float32) * inverse
            for which, value in enumerate((weighted, inverse)):
                for r in range(first, first + value.shape[0], 8):
                    for at, shift in ((r + 8, 0), (r + 8 - apart, 4)):
                        if 0 <= at <= apart + 8:
                            for block in range(blocks):
                                raw_rows[
                                    which, pl.ds(at * 8 + shift + block, 8, stride=8), :
                                ] = value[
                                    r - first : r - first + 8,
                                    block * LANES : (block + 1) * LANES,
                                ]
        ok = usable[e].astype(jnp.float32)
        ok_last = jnp.where(low, ok, jnp.where(has_below, ok, 0.0))
        for which in (0, 1):
            def tap(ref, a):
                value = ref[e, a]
                return value * value if which else value

            filtered = tap(row_taps, 0) * raw[which, pl.ds(8 - radius, apart)]
            for a in range(1, taps):
                filtered += tap(row_taps, a) * raw[which, pl.ds(8 - radius + a, apart)]
            after, before = next_blocks(filtered), previous_blocks(filtered)
            result = tap(col_taps, radius) * filtered
            for d in range(1, radius + 1):
                right = pltpu.roll(choose(lane >= d, filtered, after), LANES - d, axis=2)
                left = pltpu.roll(choose(lane >= LANES - d, before, filtered), d, axis=2)
                result += tap(col_taps, radius + d) * right + tap(col_taps, radius - d) * left
            result = result.astype(jnp.bfloat16).astype(jnp.float32)
            inside = rows - apart
            result = jnp.concatenate([result[:inside] * ok, result[inside:] * ok_last], axis=0)
            step = apart - half
            table = jnp.concatenate(
                [
                    choose(low, result[:step], roll4(result[half:])),
                    choose(low, result[step:], result[:half]),
                    choose(low, roll4(result[:inside]), result[half : half + inside]),
                ],
                axis=0,
            )
            for copy, value in enumerate((previous_blocks(table), table, next_blocks(table))):
                maps[which, pl.ds(copy * span + e * rows, rows)] = value

        for velocity in range(vels):
            for which in (0, 1):
                for start in range(0, half, 8):
                    stacks[velocity, which, pl.ds(start, 8)] += window(e, velocity, which, start)

    def put(stage, g, v, start, signal, depth):
        for base, value in (
            (start, jnp.where(low, signal, roll4(depth))),
            (start + half, jnp.where(low, roll4(signal), depth)),
        ):
            for part in range(8 // own):
                owner = base // own + part
                sums[stage][g, owner % 2, owner // 2, v] = value[part * own : (part + 1) * own]

    def get_rows(g, start):
        return jnp.concatenate(
            [
                from_code(
                    fluxes[g, (start // own + part) % 2, (start // own + part) // 2], steps
                )
                for part in range(8 // own)
            ],
            axis=0,
        ).reshape(8, 8, LANES)

    def pass_on(stage, g):
        near_copy(stage, g).wait_recv()
        mine[stage][g] = sums[stage][g, core, chip] + near[stage][g, chip]
        for j in others:
            there = peer(j)
            both = sums[stage][g, core, there] + near[stage][g, there]
            pair[stage][g, there] = to_code(both.reshape(2, own * 8, LANES), steps)
            far_copy(stage, g, j).start()

    def total(stage, g):
        value = mine[stage][g]
        for j in others:
            far_copy(stage, g, j).wait_recv()
            value = value + from_code(far[stage][g, j - 1], steps).reshape(value.shape)
        return value

    @pl.loop(0, groups)
    def _(g):
        for v in (0, 1):
            for start in range(0, half, 8):
                put(
                    0, g, v, start,
                    stacks[2 * g + v, 0, pl.ds(start, 8)], stacks[2 * g + v, 1, pl.ds(start, 8)],
                )
        near_copy(0, g).start()

    @pl.loop(0, groups)
    def _(g):
        pass_on(0, g)

    def spread_flux(g):
        whole = total(0, g)
        flux = whole / (roll4(whole) + 1.0)
        flux = jnp.where(low, flux[0], roll4(flux[1])).reshape(own * 8, LANES)
        fluxes[g, core, chip] = to_code(flux, steps)
        for j in others:
            flux_copy(g, j).start()

    def share_flux(g):
        for j in others:
            flux_copy(g, j).wait_recv()
        flux_sibling(g).start()

    def reweight(g):
        flux_sibling(g).wait_recv()
        for start in range(0, half, 8):
            upper, lower = get_rows(g, start), get_rows(g, start + half)
            for v in (0, 1):
                if v == 0:
                    flux = jnp.where(low, upper, roll4(lower))
                else:
                    flux = jnp.where(low, roll4(upper), lower)
                signal_sum = jnp.zeros((8, 8, LANES), jnp.float32)
                depth_sum = jnp.zeros((8, 8, LANES), jnp.float32)
                for e in range(exposures):
                    signal = window(e, 2 * g + v, 0, start)
                    depth = window(e, 2 * g + v, 1, start)
                    residual = signal - flux * depth
                    more = depth + 1.0
                    bottom = more + residual * residual
                    guess = pl.reciprocal(bottom, approx=True)
                    weight = more * (guess * (2.0 - bottom * guess))
                    signal_sum += weight * signal
                    depth_sum += weight * depth
                put(1, g, v, start, signal_sum, depth_sum)
        near_copy(1, g).start()

    @pl.loop(0, groups)
    def _(g):
        spread_flux(g)

    @pl.loop(0, groups + 2)
    def _(i):
        @pl.when(i < groups)
        def _():
            share_flux(i)

        @pl.when((i >= 1) & (i < groups + 1))
        def _():
            reweight(i - 1)

        @pl.when(i >= 2)
        def _():
            pass_on(1, i - 2)

    @pl.loop(0, groups)
    def _(g):
        whole = total(1, g)
        result = whole / jnp.sqrt(roll4(whole) + 1.0)
        final[...] = result.reshape(2 * own * 8, LANES)
        for v in (0, 1):
            for block in range(blocks):
                out[2 * g + v, :, block * LANES : (block + 1) * LANES] = final[
                    pl.ds(v * own * 8 + block, own, stride=8), :
                ]

    @pl.loop(0, groups)
    def _(g):
        for stage in (0, 1):
            near_copy(stage, g).wait_send()
            for j in others:
                far_copy(stage, g, j).wait_send()
        for j in others:
            flux_copy(g, j).wait_send()
        flux_sibling(g).wait_send()

    @pl.when(has_below)
    def _():
        for t in range(tiles):
            for array in (0, 1):
                edge_copy(t, array, 1).wait_send()

    @pl.when(has_above)
    def _():
        for t in range(tiles):
            for array in (0, 1):
                edge_copy(t, array, 0).wait_send()

        @pl.loop(0, exposures)
        def _(e):
            for array in (0, 1):
                full_copy(e, array).wait_send()


def per_device(count, strips, science, inv_var, psf_rows, psf_cols, row_shift, col_shift, ok):
    exposures, rows, columns = science.shape
    vels, taps = row_shift.shape[1], psf_rows.shape[1]
    chips, own, groups = count // 2, rows // count, vels // 2
    f32, bf16 = jnp.float32, jnp.bfloat16
    dma = lambda *shape: [pltpu.SemaphoreType.DMA(shape)] * 2
    radius = taps // 2
    tiles = exposures * radius // 16
    stage = [
        pltpu.VMEM((groups, 2, chips, 2, own, 8, LANES), f32),
        pltpu.VMEM((groups, chips, 2, own, 8, LANES), f32),
        pltpu.VMEM((groups, 2, own, 8, LANES), f32),
        pltpu.VMEM((groups, chips, 2, own * 8, LANES), jnp.int16),
        pltpu.VMEM((groups, chips - 1, 2, own * 8, LANES), jnp.int16),
    ]
    result = pl.pallas_call(
        functools.partial(kernel, (count, strips, exposures, rows, columns, vels, taps)),
        out_shape=jax.ShapeDtypeStruct((vels, own, columns), f32),
        in_specs=[pl.BlockSpec(memory_space=pl.ANY)] * 7,
        out_specs=pl.BlockSpec(memory_space=pltpu.VMEM),
        scratch_shapes=[
            pltpu.SMEM(psf_rows.shape, f32),
            pltpu.SMEM(psf_cols.shape, f32),
            pltpu.SMEM(row_shift.shape, jnp.int32),
            pltpu.SMEM(col_shift.shape, jnp.int32),
            pltpu.SMEM(ok.shape, jnp.int32),
            pltpu.VMEM(science.shape, bf16),
            pltpu.VMEM(science.shape, bf16),
            pltpu.SemaphoreType.DMA((7,)),
            pltpu.VMEM((2, exposures, SHIFT, columns), bf16),
            pltpu.VMEM((2, tiles, 16, columns), bf16),
            pltpu.VMEM((2, tiles, 16, columns), bf16),
            pltpu.VMEM((2, 2, tiles, 16, columns), bf16),
            pltpu.VMEM((2, 2, 16 // radius, 8, columns), f32),
            pltpu.VMEM((2, (rows + SHIFT) // 2 + 16, 8, LANES), f32),
            pltpu.VMEM((2, 3 * exposures * rows, 8, LANES), f32),
            pltpu.VMEM((vels, 2, rows // 2, 8, LANES), f32),
            pltpu.VMEM((groups, 2, chips, own * 8, LANES), jnp.int16),
            pltpu.VMEM((2 * own * 8, LANES), f32),
            *stage,
            *stage,
            *dma(2, exposures),
            *dma(2, 2, tiles),
            *dma(2, groups),
            *dma(2, groups, chips - 1),
            *dma(groups, chips - 1),
            *dma(groups),
        ],
        compiler_params=pltpu.CompilerParams(
            collective_id=0, has_side_effects=True, vmem_limit_bytes=24 * 1024 * 1024
        ),
    )(
        *(
            pltpu.with_memory_space_constraint(x, pltpu.HBM)
            for x in (psf_rows, psf_cols, row_shift, col_shift, ok, science, inv_var)
        )
    )
    return result.reshape(1, vels, own, columns)


def solution(mesh):
    from jax.sharding import PartitionSpec as P

    in_specs = (
        P(("field", "expo"), "strip", None),
        P(("field", "expo"), "strip", None),
        P(("field", "expo"), None),
        P(("field", "expo"), None),
        P(("field", "expo"), None),
        P(("field", "expo"), None),
        P(("field", "expo")),
    )
    return jax.shard_map(
        functools.partial(per_device, mesh.shape["expo"], mesh.shape["strip"]),
        mesh=mesh,
        in_specs=in_specs,
        out_specs=P("strip", "field", "expo", None),
        check_vma=False,
    )
```
